256 devices in a mesh: section: 4 (over y), dp: 16 (over z_hi, x), tensor: 4 (over z_lo, core).
Axes of the slice: x: 4, y: 4, z: 8 (z_hi: 4, z_lo: 2; z = z_hi * 2 + z_lo), core: 2. Of those that a mesh axis runs over, the one named last changes fastest.
Arguments:
- states: bfloat16 [32, 128, 8192], P('dp', None, ('section', 'tensor')), may hold values from -60 to 60
- gain: bfloat16 [8192], P(('section', 'tensor')), may hold values from 0.25 to 1.75
- kv_weight: bfloat16 [4, 8192, 2, 2048], P('section', 'dp', None, 'tensor'), may hold values from -0.0625 to 0.0625
- queries: bfloat16 [4, 32, 256, 2048], P('section', 'dp', None, 'tensor'), may hold values from -6 to 6
- out_grad: bfloat16 [4, 32, 256, 2048], P('section', 'dp', None, 'tensor'), may hold values from -24 to 24
- src_len: int32 [32], P('dp'), may hold values from 32 to 128, as said below
Outputs:
- attended: bfloat16 [4, 32, 256, 2048], P('section', 'dp', None, 'tensor')
- grad_queries: bfloat16 [4, 32, 256, 2048], P('section', 'dp', None, 'tensor')
- grad_states: float32 [32, 128, 8192], P('dp', None, ('section', 'tensor'))
- grad_gain: float32 [8192], P(('section', 'tensor'))
The draws below stay inside these ranges and needn't reach their ends.
Inputs may be any that keep to these rules, and one draw needn't show every extreme that they name: `src_len`: the largest value 128 is reached.
All inputs are finite; a program needn't handle non-finite values.
Results may differ from the reference program's by a relative error of at most 0.0095.
Values may be sent and summed in bfloat16 or wider, within the bound.
A program may use at most 128 MiB of HBM per device.

```python
import jax
import jax.numpy as jnp
from jax import lax

D = 8192
HEADS = 32
HEAD_DIM = 64
SRC = 128
TGT = 256
HC = 2048
BATCH = 32
N_SECTION = 4


def draw_states(key, part):
    key = jax.random.fold_in(key, 2)
    base_key, row_key = jax.random.split(key)
    base = jnp.clip(jax.random.normal(base_key, (BATCH, SRC, D), jnp.float32), -4.0, 4.0)
    rows = jnp.exp(jax.random.uniform(row_key, (BATCH, SRC, 1), jnp.float32, 0.0, 2.302585))
    columns = jnp.linspace(0.5, 1.5, D, dtype=jnp.float32)
    return (base * rows * columns).astype(jnp.bfloat16)


def draw_src_len(key, part):
    key = jax.random.fold_in(key, 1)
    lengths = jax.random.randint(key, (BATCH,), SRC // 4, SRC + 1, jnp.int32)
    return lengths.at[0].set(SRC)


def steps_of(rng, shape, cuts, low, high):
    loudness, own = 1.0, jax.random.fold_in(rng, 6)
    for axis_at, parts in cuts:
        steps = jnp.exp(jax.random.uniform(jax.random.fold_in(own, axis_at), (parts,), jnp.float32, low / len(cuts), high / len(cuts)))
        loudness = loudness * jnp.repeat(steps, shape[axis_at] // parts).reshape([-1 if axis == axis_at else 1 for axis in range(len(shape))])
    return loudness


def bell_draw(rng, extent, scale, bound, cuts=(), kind=jnp.bfloat16):
    loudness = steps_of(rng, extent, cuts, -0.22, 0.18) if cuts else 1.0
    array = jax.random.normal(rng, extent, jnp.float32) * scale * loudness
    return jnp.minimum(jnp.maximum(array, -bound), bound).astype(kind)


def setup_inputs(seed: int = 0) -> dict:
    key_list = jax.random.split(jax.random.key(seed), 7)
    return {
        "states": draw_states(jax.random.fold_in(key_list[6], 71), 0),
        "gain": jnp.clip(1.0 + 0.15 * jax.random.normal(key_list[1], (D,), jnp.float32), 0.25, 1.75).astype(jnp.bfloat16),
        "kv_weight": bell_draw(key_list[2], (N_SECTION, D, 2, HC), D ** -0.5, 0.0625, ((0, 4), (1, 16), (3, 4))),
        "queries": bell_draw(key_list[3], (N_SECTION, BATCH, TGT, HC), 1.0, 6.0, ((0, 4), (1, 16), (3, 4))),
        "out_grad": bell_draw(key_list[4], (N_SECTION, BATCH, TGT, HC), 4.0, 24.0, ((0, 4), (1, 16), (3, 4))),
        "src_len": draw_src_len(jax.random.fold_in(key_list[6], 71), 0),
    }


def reference(states, gain, kv_weight, queries, out_grad, src_len):
    hf = states.astype(jnp.float32)
    gf = gain.astype(jnp.float32)
    inv = 1.0 / jnp.sqrt(lax.optimization_barrier(jnp.mean(hf * hf, axis=-1)) + 1e-06)
    normed = (hf * inv[..., None] * gf).astype(jnp.bfloat16)
    valid = jnp.arange(SRC, dtype=jnp.int32)[None, :] < src_len[:, None]
    scale = HEAD_DIM ** (-0.5)
    attended_all = []
    grad_q_all = []
    dnormed = jnp.zeros(hf.shape, jnp.float32)
    for section in range(N_SECTION):
        kv = jnp.einsum('bsd,dch->bsch', normed.astype(jnp.float32), kv_weight[section].astype(jnp.float32)).astype(jnp.bfloat16)
        keys = kv[:, :, 0].reshape(BATCH, SRC, HEADS, HEAD_DIM).astype(jnp.float32)
        values = kv[:, :, 1].reshape(BATCH, SRC, HEADS, HEAD_DIM).astype(jnp.float32)
        query = queries[section].reshape(BATCH, TGT, HEADS, HEAD_DIM).astype(jnp.float32)
        cotan = out_grad[section].reshape(BATCH, TGT, HEADS, HEAD_DIM).astype(jnp.float32)
        scores = jnp.einsum('bthe,bshe->bhts', query, keys) * scale
        expo = jnp.where(valid[:, None, None, :], jnp.exp(scores), 0.0)
        probs = expo / lax.optimization_barrier(jnp.sum(expo, axis=-1, keepdims=True))
        probs_b = probs.astype(jnp.bfloat16).astype(jnp.float32)
        attended_all.append(jnp.einsum('bhts,bshe->bthe', probs_b, values).astype(jnp.bfloat16).reshape(BATCH, TGT, HC))
        dprob = jnp.einsum('bthe,bshe->bhts', cotan, values)
        delta = lax.optimization_barrier(jnp.sum(probs * dprob, axis=-1, keepdims=True))
        dscore = (probs * (dprob - delta) * scale).astype(jnp.bfloat16).astype(jnp.float32)
        grad_q_all.append(jnp.einsum('bhts,bshe->bthe', dscore, keys).astype(jnp.bfloat16).reshape(BATCH, TGT, HC))
        dkey = jnp.einsum('bhts,bthe->bshe', dscore, query).astype(jnp.bfloat16).reshape(BATCH, SRC, HC)
        dvalue = jnp.einsum('bhts,bthe->bshe', probs_b, cotan).astype(jnp.bfloat16).reshape(BATCH, SRC, HC)
        dkv = jnp.stack([dkey, dvalue], axis=2).astype(jnp.float32)
        dnormed = dnormed + jnp.einsum('bsch,dch->bsd', dkv, kv_weight[section].astype(jnp.float32))
    rowdot = lax.optimization_barrier(jnp.sum(dnormed * hf * gf, axis=-1))
    grad_states = gf * inv[..., None] * dnormed - hf * (rowdot * inv * inv * inv)[..., None] / D
    grad_gain = lax.optimization_barrier(jnp.sum(dnormed * hf * inv[..., None], axis=(0, 1)))
    return (jnp.stack(attended_all), jnp.stack(grad_q_all), grad_states, grad_gain)
```

```python
import jax
import jax.numpy as jnp
from jax import lax
from jax.experimental import pallas as pl
from jax.experimental.pallas import tpu as pltpu
from jax.sharding import PartitionSpec as P

MESH = pl.DeviceIdType.MESH
HEAD_DIM = 64
SCALE = HEAD_DIM ** (-0.5)
EPS = 1e-06
MASKED = -1e30
NX, NY, NZ = 4, 4, 4
CHUNKS = 4
F32, BF16 = jnp.float32, jnp.bfloat16


def rotate(a, by, n):
    return lax.rem(a + by, n)


def kernel(
    w_ref, states_ref, gain_ref, q_ref, og_ref, bias_ref,
    att_ref, gq_ref, gs_ref, gg_ref,
    hg, wg, a, own_part, part_send, rs_recv, ag, dn, core_send, core_recv, y_send, y_recv, y_own,
    fin_send, fin, kvf, racc, small, gsum, inv_ref, rsum_ref,
    local_sem, wd_s, wd_r, wf_s, wf_r, s1_s, s1_r, s2_s, s2_r, s3_s, s3_r, rs_s, rs_r, ag_s, ag_r,
    d1_s, d1_r, d2_s, d2_r, d3_s, d3_r, sm_s, sm_r, gs_s, gs_r,
):
    y, d, t = lax.axis_index("section"), lax.axis_index("dp"), lax.axis_index("tensor")
    zh, x, zl, core = d // 4, lax.rem(d, 4), t // 2, lax.rem(t, 2)
    rows, feats = states_ref.shape
    batches = q_ref.shape[0]
    src = rows // batches
    cols = w_ref.shape[2]

    def at(y_=None, zh_=None, x_=None, zl_=None, core_=None):
        pick = lambda new, old: old if new is None else new
        return (pick(y_, y), pick(zh_, zh) * 4 + pick(x_, x), pick(zl_, zl) * 2 + pick(core_, core))

    def copy(src_ref, dst_ref, send, recv, to):
        return pltpu.make_async_remote_copy(
            src_ref=src_ref, dst_ref=dst_ref, send_sem=send, recv_sem=recv, device_id=to, device_id_type=MESH
        )

    other = 1 - core
    home = t == x

    barrier = pltpu.get_barrier_semaphore()

    def greet(to):
        pl.semaphore_signal(barrier, inc=1, device_id=to, device_id_type=MESH)

    for k in (1, 2, 3):
        greet(at(zh_=rotate(zh, k, NZ)))
        greet(at(y_=rotate(y, k, NY)))
        greet(at(x_=rotate(x, k, NX)))
    greet(at(core_=other))
    greet(at(zl_=1 - zl))
    x_core = lax.rem(x, 2)
    greet(at(x_=t, zl_=1 - zl, core_=x_core))
    source = lambda half: (y, zh * 4 + core + 2 * half, x)
    far_half = jnp.where(home, 1 - x // 2, 0)

    @pl.when(jnp.logical_not(home))
    def _():
        greet(at(x_=t, core_=x_core))
        greet(source(0))
        greet(source(1))
        pl.semaphore_wait(barrier, 15)

    @pl.when(home)
    def _():
        greet(source(far_half))
        pl.semaphore_wait(barrier, 13)

    def w_direct(c, up):
        to = at(zh_=rotate(zh, 1 if up else 3, NZ))
        return copy(w_ref.at[c], wg.at[3 if up else 1, c], wd_s.at[int(up), c], wd_r.at[int(up), c], to)

    def w_forward(c, up):
        half = feats // 2
        part = pl.ds(0 if up else half, half)
        to = at(zh_=rotate(zh, 1 if up else 3, NZ))
        return copy(
            wg.at[3 if up else 1, c, part], wg.at[2, c, part], wf_s.at[int(up), c], wf_r.at[int(up), c], to
        )

    def pump(c):
        for up in (True, False):
            w_direct(c, up).wait_recv()
            w_forward(c, up).start()

    def w_send(c):
        for up in (True, False):
            w_direct(c, up).start()

    own_w = pltpu.make_async_copy(w_ref, wg.at[0], local_sem.at[0])
    own_w.start()
    w_send(0)

    h = states_ref[...].astype(F32)
    hg[...] = (h * gain_ref[...]).astype(BF16)
    squares = h * h

    def s1_copy(z, to):
        return copy(hg, a.at[x, y], s1_s.at[z], s1_r.at[x // 2], to)

    s1_far = s1_copy(1, at(x_=t, zl_=1 - zl, core_=x_core))
    s1_near = s1_copy(0, at(x_=t, core_=x_core))
    s1_local = pltpu.make_async_copy(hg, a.at[x, y], s1_r.at[x // 2])
    s1_far.start()

    @pl.when(jnp.logical_not(home))
    def _():
        s1_near.start()

    @pl.when(home)
    def _():
        s1_local.start()

    w_send(1)

    def total_lanes(v):
        acc = v[:, :128]
        for k in range(128, v.shape[1], 128):
            acc = acc + v[:, k : k + 128]
        return jnp.broadcast_to(jnp.sum(acc.T, axis=0, keepdims=True), (8, rows))

    def spread(row):
        return jnp.broadcast_to(row, (128, rows)).T

    def reduce_start(base, v):
        small[base] = v
        c = copy(small.at[base], small.at[base + 1], sm_s.at[base], sm_r.at[base + 1], at(core_=other))
        c.start()

    def reduce_zl(base):
        copy(small.at[base], small.at[base + 1], sm_s.at[base], sm_r.at[base + 1], at(core_=other)).wait()
        small[base + 2] = small[base] + small[base + 1]
        copy(small.at[base + 2], small.at[base + 3], sm_s.at[base + 2], sm_r.at[base + 3], at(zl_=1 - zl)).start()

    def reduce_y_copies(base):
        return [
            copy(
                small.at[base + 4], small.at[base + 4 + k], sm_s.at[base + 4 + k], sm_r.at[base + 4 + k],
                at(y_=rotate(y, k, NY)),
            )
            for k in (1, 2, 3)
        ]

    def reduce_y(base):
        copy(small.at[base + 2], small.at[base + 3], sm_s.at[base + 2], sm_r.at[base + 3], at(zl_=1 - zl)).wait()
        small[base + 4] = small[base + 2] + small[base + 3]
        for c in reduce_y_copies(base):
            c.start()

    def reduce_end(base):
        for c in reduce_y_copies(base):
            c.wait()
        return (small[base + 4] + small[base + 5]) + (small[base + 6] + small[base + 7])

    reduce_start(0, total_lanes(squares))

    def s2_copy(half, k):
        piece = a.at[core + 2 * half, y]
        return copy(piece, piece, s2_s.at[half, k - 1], s2_r.at[half, k - 1], at(y_=rotate(y, k, NY)))

    def s2_arrival(half, k):
        piece = a.at[core + 2 * half, rotate(y, 4 - k, NY)]
        return copy(piece, piece, s2_s.at[half, k - 1], s2_r.at[half, k - 1], at(y_=rotate(y, k, NY)))

    def s3_copy(half, k):
        piece = a.at[core + 2 * half, rotate(y, 4 - k, NY)]
        return copy(piece, piece, s3_s.at[half, k], s3_r.at[half, k], at(core_=other))

    def s3_arrival(half, k):
        piece = a.at[other + 2 * half, rotate(y, 4 - k, NY)]
        return copy(piece, piece, s3_s.at[half, k], s3_r.at[half, k], at(core_=other))

    for half in (0, 1):
        copy(hg, a.at[core + 2 * half, y], s1_s.at[0], s1_r.at[half], at(core_=other)).wait_recv()
        for k in (1, 3, 2):
            s2_copy(half, k).start()
    for half in (0, 1):
        s3_copy(half, 0).start()
    reduce_zl(0)
    pump(0)
    w_send(2)
    reduce_y(0)
    pump(1)
    w_send(3)
    for half in (0, 1):
        for k in (1, 3, 2):
            s2_arrival(half, k).wait_recv()
            s3_copy(half, k).start()
    total = reduce_end(0)
    inv = 1.0 / jnp.sqrt(spread(total[:1]) / (NX * NZ * feats) + EPS)
    inv_ref[...] = inv
    racc[...] = jnp.zeros_like(racc)
    for half in (0, 1):
        for k in range(4):
            s3_arrival(half, k).wait_recv()
    own_w.wait()

    def rs_copy(c, j):
        return copy(part_send.at[c, j], rs_recv.at[c, j], rs_s.at[c, j], rs_r.at[c, j], at(x_=rotate(x, 1 + j, NX)))

    def ag_copy(c, j):
        return copy(ag.at[c, x], ag.at[c, x], ag_s.at[c, j], ag_r.at[c, j], at(x_=rotate(x, 1 + j, NX)))

    def ag_arrival(c, j):
        piece = ag.at[c, rotate(x, 3 - j, NX)]
        return copy(piece, piece, ag_s.at[c, j], ag_r.at[c, j], at(x_=rotate(x, 1 + j, NX)))

    def project(c):
        for up in (True, False):
            w_forward(c, up).wait_recv()

        def one(j):
            xs = rotate(x, 1 + j, NX)
            acc = jnp.zeros((rows, cols), F32)
            for r in range(4):
                acc = acc + jnp.dot(a[xs, rotate(zh, r, NZ)], wg[r, c], preferred_element_type=F32)
            return acc

        def send(j, carry):
            part_send[c, j] = one(j).astype(BF16)
            rs_copy(c, j).start()
            return carry

        lax.fori_loop(0, 3, send, 0)
        own_part[c] = one(3)

    lane = lax.broadcasted_iota(jnp.int32, (1, 128), 1)
    first = lane < HEAD_DIM

    def two_heads(v):
        return jnp.concatenate([jnp.where(first, v, 0.0), jnp.where(first, 0.0, v)], axis=0).astype(BF16)

    def per_head(v, f):
        return jnp.concatenate([f(v[:, :src]), f(v[:, src:])], axis=1)

    def dot_t(m, n):
        return lax.dot_general(m, n, (((1,), (1,)), ((), ())), preferred_element_type=F32)

    def t_dot(m, n):
        return lax.dot_general(m, n, (((0,), (0,)), ((), ())), preferred_element_type=F32)

    def attend(c):
        for j in range(3):
            rs_copy(c, j).wait_recv()
        kv = own_part[c]
        for j in range(3):
            kv = kv + rs_recv[c, j].astype(F32)
        kvf[...] = kv * jnp.concatenate([inv_ref[...]] * (cols // 128), axis=1)
        lanes = pl.ds(pl.multiple_of(c * 128, 128), 128)

        def one(b, carry):
            at_rows = pl.ds(pl.multiple_of(b * src, src), src)
            kv_b = kvf[at_rows, :]
            keys = two_heads(kv_b[:, :128].astype(BF16).astype(F32))
            values = two_heads(kv_b[:, 128:].astype(BF16).astype(F32))
            query, cotan = q_ref[b, :, lanes], og_ref[b, :, lanes]
            expo = jnp.exp(dot_t(query, keys) * SCALE + bias_ref[b, :1, :])
            probs = per_head(expo, lambda e: e / jnp.sum(e, axis=-1, keepdims=True))
            probs_b = probs.astype(BF16)
            att_ref[b, :, lanes] = jnp.dot(probs_b, values, preferred_element_type=F32).astype(BF16)
            dprob = dot_t(cotan, values)
            delta = per_head(
                probs * dprob, lambda e: jnp.broadcast_to(jnp.sum(e, axis=-1, keepdims=True), e.shape)
            )
            dscore = (probs * (dprob - delta) * SCALE).astype(BF16)
            gq_ref[b, :, lanes] = jnp.dot(dscore, keys, preferred_element_type=F32).astype(BF16)
            dkey, dvalue = t_dot(dscore, query), t_dot(probs_b, cotan)
            dkv = jnp.concatenate(
                [jnp.where(first, dkey[:src], dkey[src:]), jnp.where(first, dvalue[:src], dvalue[src:])], axis=1
            ).astype(BF16)
            ag[c, x, at_rows, :] = dkv
            product = dkv.astype(F32) * kv_b
            racc[at_rows, :] = racc[at_rows, :] + (product[:, :128] + product[:, 128:])
            return carry

        lax.fori_loop(0, batches, one, 0)
        for j in range(3):
            ag_copy(c, j).start()

    def back(c):
        for j in range(3):
            ag_arrival(c, j).wait_recv()

        def one(i, carry):
            xs, r = i // 4, lax.rem(i, 4)
            term = dot_t(ag[c, xs], wg[r, c])

            @pl.when(c == 0)
            def _():
                dn[xs, r] = term

            @pl.when(c > 0)
            def _():
                dn[xs, r] = dn[xs, r] + term

            return carry

        lax.fori_loop(0, 16, one, 0)

    def turn(i, carry):
        @pl.when(i < CHUNKS)
        def _():
            project(i)

        @pl.when(i + 2 < CHUNKS)
        def _():
            pump(i + 2)

        @pl.when(jnp.logical_and(i >= 1, i <= CHUNKS))
        def _():
            attend(i - 1)

        @pl.when(i >= 2)
        def _():
            back(i - 2)

        return carry

    lax.fori_loop(0, CHUNKS + 1, turn, 0)
    reduce_start(8, total_lanes(racc[...]))
    back(CHUNKS - 1)

    def d1_copy(half, r):
        return copy(core_send.at[half, r], core_recv.at[half, r], d1_s.at[half, r], d1_r.at[half, r], at(core_=other))

    def d1_send(i, carry):
        half, r = i // 4, lax.rem(i, 4)
        core_send[half, r] = dn[other + 2 * half, r].astype(BF16)
        d1_copy(half, r).start()
        return carry

    lax.fori_loop(0, 8, d1_send, 0)
    reduce_zl(8)

    def d2_copy(half, k):
        return copy(
            y_send.at[half, k - 1], y_recv.at[half, k - 1], d2_s.at[half, k - 1], d2_r.at[half, k - 1],
            at(y_=rotate(y, k, NY)),
        )

    def chip_sum(half, r):
        d1_copy(half, r).wait_recv()
        return dn[core + 2 * half, r] + core_recv[half, r].astype(F32)

    def d2_send(i, carry):
        half, k = i // 3, lax.rem(i, 3) + 1
        y_send[half, k - 1] = chip_sum(half, lax.rem(y + k + NZ - zh, NZ)).astype(BF16)
        d2_copy(half, k).start()
        return carry

    lax.fori_loop(0, 6, d2_send, 0)
    for half in (0, 1):
        y_own[half] = chip_sum(half, lax.rem(y + NZ - zh, NZ))
    reduce_y(8)
    total = reduce_end(8)
    inv = inv_ref[...]
    rsum_ref[...] = spread(total[:1]) * inv * inv / (NX * NZ * feats)

    def d3_copy(half):
        to = (y, zh * 4 + core + 2 * half, x)
        return copy(fin_send.at[half], fin.at[zl], d3_s.at[half], d3_r.at[zl], to)

    for half in (0, 1):
        for k in (1, 2, 3):
            d2_copy(half, k).wait_recv()
        v = y_own[half]
        for k in range(3):
            v = v + y_recv[half, k].astype(F32)
        fin_send[half] = v.astype(BF16)
        stays = jnp.logical_and(home, x // 2 == half)

        @pl.when(stays)
        def _():
            pltpu.make_async_copy(fin_send.at[half], fin.at[zl], d3_r.at[zl]).start()

        @pl.when(jnp.logical_not(stays))
        def _():
            d3_copy(half).start()

    for k in (0, 1):
        copy(fin_send.at[0], fin.at[k], d3_s.at[0], d3_r.at[k], at(core_=other)).wait_recv()
    dnormed = fin[0].astype(F32) + fin[1].astype(F32)
    h = states_ref[...].astype(F32)
    wide = lambda v: jnp.concatenate([v] * (feats // 128), axis=1)
    inv = wide(inv_ref[...])
    scaled = dnormed * inv

    def gain_copy(over_x, k):
        piece = gsum.at[x] if over_x else gsum.at[4 + zh]
        place = k if over_x else 4 + k
        to = at(x_=rotate(x, k, NX)) if over_x else at(zh_=rotate(zh, k, NZ))
        return copy(piece, piece, gs_s.at[place], gs_r.at[place], to)

    def gain_arrival(over_x, k):
        piece = gsum.at[rotate(x, 4 - k, NX)] if over_x else gsum.at[4 + rotate(zh, 4 - k, NZ)]
        place = k if over_x else 4 + k
        to = at(x_=rotate(x, k, NX)) if over_x else at(zh_=rotate(zh, k, NZ))
        return copy(piece, piece, gs_s.at[place], gs_r.at[place], to)

    gsum[x] = jnp.broadcast_to(jnp.sum(scaled * h, axis=0, keepdims=True), (8, feats))
    for k in (1, 2, 3):
        gain_copy(True, k).start()
    gs_ref[...] = gain_ref[...] * scaled - h * wide(rsum_ref[...])
    for k in (1, 2, 3):
        gain_arrival(True, k).wait_recv()
    gsum[4 + zh] = (gsum[0] + gsum[1]) + (gsum[2] + gsum[3])
    for k in (1, 2, 3):
        gain_copy(False, k).start()

    def sent_w(c, carry):
        for up in (True, False):
            w_direct(c, up).wait_send()
            w_forward(c, up).wait_send()
        for j in range(3):
            rs_copy(c, j).wait_send()
            ag_copy(c, j).wait_send()
        return carry

    lax.fori_loop(0, CHUNKS, sent_w, 0)
    s1_far.wait_send()

    @pl.when(jnp.logical_not(home))
    def _():
        s1_near.wait_send()

    for half in (0, 1):
        for k in (1, 2, 3):
            s2_copy(half, k).wait_send()
            d2_copy(half, k).wait_send()
        for k in range(4):
            s3_copy(half, k).wait_send()
            d1_copy(half, k).wait_send()

        @pl.when(jnp.logical_not(jnp.logical_and(home, x // 2 == half)))
        def _():
            d3_copy(half).wait_send()

    for k in (1, 2, 3):
        gain_copy(True, k).wait_send()
    for k in (1, 2, 3):
        gain_arrival(False, k).wait_recv()
    gg_ref[...] = (gsum[4] + gsum[5]) + (gsum[6] + gsum[7])
    for k in (1, 2, 3):
        gain_copy(False, k).wait_send()


def per_device(states, gain, kv_weight, queries, out_grad, src_len):
    batches, src, feats = states.shape
    tgt, heads_cols = queries.shape[2:]
    rows = batches * src
    cols = 2 * heads_cols // CHUNKS
    w = kv_weight[0].reshape(feats, 2, CHUNKS, cols // 2).transpose(2, 0, 1, 3).reshape(CHUNKS, feats, cols)
    valid = jnp.arange(src, dtype=jnp.int32)[None, :] < src_len[:, None]
    bias = jnp.where(valid, 0.0, MASKED).astype(F32)
    bias = jnp.broadcast_to(jnp.concatenate([bias, bias], axis=1)[:, None, :], (batches, 8, 2 * src))
    vmem = pl.BlockSpec(memory_space=pltpu.VMEM)
    dma = pltpu.SemaphoreType.DMA
    out = pl.pallas_call(
        kernel,
        out_shape=(
            jax.ShapeDtypeStruct((batches, tgt, heads_cols), BF16),
            jax.ShapeDtypeStruct((batches, tgt, heads_cols), BF16),
            jax.ShapeDtypeStruct((rows, feats), F32),
            jax.ShapeDtypeStruct((8, feats), F32),
        ),
        in_specs=[vmem] * 6,
        out_specs=[vmem] * 4,
        scratch_shapes=[
            pltpu.VMEM((rows, feats), BF16),
            pltpu.VMEM((4, CHUNKS, feats, cols), BF16),
            pltpu.VMEM((4, 4, rows, feats), BF16),
            pltpu.VMEM((CHUNKS, rows, cols), F32),
            pltpu.VMEM((CHUNKS, 3, rows, cols), BF16),
            pltpu.VMEM((CHUNKS, 3, rows, cols), BF16),
            pltpu.VMEM((CHUNKS, 4, rows, cols), BF16),
            pltpu.VMEM((4, 4, rows, feats), F32),
            pltpu.VMEM((2, 4, rows, feats), BF16),
            pltpu.VMEM((2, 4, rows, feats), BF16),
            pltpu.VMEM((2, 3, rows, feats), BF16),
            pltpu.VMEM((2, 3, rows, feats), BF16),
            pltpu.VMEM((2, rows, feats), F32),
            pltpu.VMEM((2, rows, feats), BF16),
            pltpu.VMEM((2, rows, feats), BF16),
            pltpu.VMEM((rows, cols), F32),
            pltpu.VMEM((rows, 128), F32),
            pltpu.VMEM((16, 8, rows), F32),
            pltpu.VMEM((8, 8, feats), F32),
            pltpu.VMEM((rows, 128), F32),
            pltpu.VMEM((rows, 128), F32),
            dma((1,)),
            dma((2, CHUNKS)), dma((2, CHUNKS)), dma((2, CHUNKS)), dma((2, CHUNKS)),
            dma((2,)), dma((2,)),
            dma((2, 3)), dma((2, 3)),
            dma((2, 4)), dma((2, 4)),
            dma((CHUNKS, 3)), dma((CHUNKS, 3)),
            dma((CHUNKS, 3)), dma((CHUNKS, 3)),
            dma((2, 4)), dma((2, 4)),
            dma((2, 3)), dma((2, 3)),
            dma((2,)), dma((2,)),
            dma((16,)), dma((16,)),
            dma((8,)), dma((8,)),
        ],
        compiler_params=pltpu.CompilerParams(
            collective_id=1, has_side_effects=True, vmem_limit_bytes=52 * 2**20
        ),
        name="cross_attention",
    )(
        w, states.reshape(rows, feats), gain.astype(F32).reshape(1, feats), queries[0], out_grad[0], bias
    )
    attended, grad_q, grad_states, grad_gain = out
    return attended[None], grad_q[None], grad_states.reshape(batches, src, feats), grad_gain[0]


def solution(mesh):
    return jax.shard_map(
        per_device,
        mesh=mesh,
        in_specs=(
            P("dp", None, ("section", "tensor")),
            P(("section", "tensor")),
            P("section", "dp", None, "tensor"),
            P("section", "dp", None, "tensor"),
            P("section", "dp", None, "tensor"),
            P("dp"),
        ),
        out_specs=(
            P("section", "dp", None, "tensor"),
            P("section", "dp", None, "tensor"),
            P("dp", None, ("section", "tensor")),
            P(("section", "tensor")),
        ),
        check_vma=False,
    )
```

```python
import jax
import jax.numpy as jnp
from jax import lax
from jax.experimental import pallas as pl
from jax.experimental.pallas import tpu as pltpu
from jax.sharding import PartitionSpec as P

MESH = pl.DeviceIdType.MESH
HEAD_DIM = 64
SCALE = HEAD_DIM ** (-0.5)
EPS = 1e-06
NX, NY, NZ = 4, 4, 4
CHUNKS = 4
F32, BF16 = jnp.float32, jnp.bfloat16


def rotate(a, by, n):
    return lax.rem(a + by, n)


def kernel(
    w_ref, ext_ref, q_in, og_in, len_ref,
    att_ref, gq_ref, gs_ref, gg_ref,
    ext, q_ref, og_ref, wg, raw, a, own_part, part_send, rs_recv, ag, dn, core_send, core_recv, z_send, z_recv, y_send, y_recv,
    y_own, fin_send, fin, racc, small, xtot, gz, gx, inv_ref, piece_inv, rsum_ref,
    local_sem, wd_s, wd_r, wf_s, wf_r, s1_s, s1_r, s2_s, s2_r, s2f_s, s2f_r, s3_s, s3_r, rs_s, rs_r, ag_s, ag_r,
    d1_s, d1_r, dz_s, dz_r, d2_s, d2_r, d3_s, d3_r, sm_s, sm_r, xt_s, xt_r, gz_s, gz_r, gx_s, gx_r,
):
    y, d, t = lax.axis_index("section"), lax.axis_index("dp"), lax.axis_index("tensor")
    zh, x, zl, core = d // 4, lax.rem(d, 4), t // 2, lax.rem(t, 2)
    rows, feats = gs_ref.shape
    batches = q_ref.shape[0]
    src = rows // batches
    cols = wg.shape[3]
    heads_cols = q_ref.shape[2]
    width = NX * NZ * feats

    def at(y_=None, zh_=None, x_=None, zl_=None, core_=None):
        pick = lambda new, old: old if new is None else new
        return (pick(y_, y), pick(zh_, zh) * 4 + pick(x_, x), pick(zl_, zl) * 2 + pick(core_, core))

    def copy(src_ref, dst_ref, send, recv, to):
        return pltpu.make_async_remote_copy(
            src_ref=src_ref, dst_ref=dst_ref, send_sem=send, recv_sem=recv, device_id=to, device_id_type=MESH
        )

    other = 1 - core
    home = t == x

    load_ext = pltpu.make_async_copy(ext_ref, ext, local_sem.at[0])
    load_q = pltpu.make_async_copy(q_in, q_ref, local_sem.at[1])
    load_og = pltpu.make_async_copy(og_in, og_ref, local_sem.at[2])
    load_ext.start()
    load_q.start()
    load_og.start()
    barrier = pltpu.get_barrier_semaphore()

    def greet(to):
        pl.semaphore_signal(barrier, inc=1, device_id=to, device_id_type=MESH)

    for k in (1, 2, 3):
        greet(at(zh_=rotate(zh, k, NZ)))
        greet(at(y_=rotate(y, k, NY)))
        greet(at(x_=rotate(x, k, NX)))
    greet(at(core_=other))
    greet(at(zl_=1 - zl))
    for zl_ in (0, 1):
        for core_ in (0, 1):
            itself = jnp.logical_and(home, jnp.logical_and(zl == zl_, core == core_))

            @pl.when(jnp.logical_not(itself))
            def _():
                greet(at(x_=t, zl_=zl_, core_=core_))

    for x_ in range(NX):

        @pl.when(jnp.logical_not(jnp.logical_and(home, x == x_)))
        def _():
            greet((y, zh * 4 + x_, x))

    @pl.when(jnp.logical_not(home))
    def _():
        pl.semaphore_wait(barrier, 19)

    @pl.when(home)
    def _():
        pl.semaphore_wait(barrier, 17)

    x_core = lax.rem(x, 2)

    def w_lanes(c):
        k = pl.ds(pl.multiple_of(c * 128, 128), 128)
        v = pl.ds(pl.multiple_of(heads_cols + c * 128, 128), 128)
        return ((k, pl.ds(0, 128)), (v, pl.ds(128, 128)))

    def w_direct(c, up):
        to = at(zh_=rotate(zh, 1 if up else 3, NZ))
        piece = wg.at[3 if up else 1, c]
        return copy(piece, piece, wd_s.at[int(up), c], wd_r.at[int(up), c], to)

    def w_forward(c, up):
        half = feats // 2
        part = pl.ds(0 if up else half, half)
        to = at(zh_=rotate(zh, 1 if up else 3, NZ))
        return copy(
            wg.at[3 if up else 1, c, part], wg.at[2, c, part], wf_s.at[int(up), c], wf_r.at[int(up), c], to
        )

    def pump(c):
        for up in (True, False):
            w_direct(c, up).wait_recv()
            w_forward(c, up).start()

    def w_send(c):
        for up in (True, False):
            to = at(zh_=rotate(zh, 1 if up else 3, NZ))
            for here, there in w_lanes(c):
                copy(
                    w_ref.at[:, here], wg.at[3 if up else 1, c, :, there],
                    wd_s.at[int(up), c], wd_r.at[int(up), c], to,
                ).start()

    load_ext.wait()

    def s1_copy(z, to):
        return copy(ext, raw.at[x // 2, y], s1_s.at[z], s1_r.at[x // 2], to)

    s1_far = s1_copy(1, at(x_=t, zl_=1 - zl, core_=x_core))
    s1_near = s1_copy(0, at(x_=t, core_=x_core))
    s1_local = pltpu.make_async_copy(ext, raw.at[x // 2, y], s1_r.at[x // 2])
    s1_far.start()

    @pl.when(jnp.logical_not(home))
    def _():
        s1_near.start()

    @pl.when(home)
    def _():
        s1_local.start()

    for c in range(CHUNKS):
        for here, there in w_lanes(c):
            pltpu.make_async_copy(w_ref.at[:, here], wg.at[0, c, :, there], local_sem.at[3]).start()

    h = ext[:rows, :].astype(F32)
    squares = h * h

    def total_lanes(v):
        acc = v[:, :128]
        for k in range(128, v.shape[1], 128):
            acc = acc + v[:, k : k + 128]
        return jnp.broadcast_to(jnp.sum(acc.T, axis=0, keepdims=True), (8, rows))

    def spread(row):
        return jnp.broadcast_to(row, (128, rows)).T

    def reduce_start(base, v):
        small[base] = v
        c = copy(small.at[base], small.at[base + 1], sm_s.at[base], sm_r.at[base + 1], at(core_=other))
        c.start()

    def reduce_zl(base):
        copy(small.at[base], small.at[base + 1], sm_s.at[base], sm_r.at[base + 1], at(core_=other)).wait()
        small[base + 2] = small[base] + small[base + 1]
        copy(small.at[base + 2], small.at[base + 3], sm_s.at[base + 2], sm_r.at[base + 3], at(zl_=1 - zl)).start()

    def reduce_y_copies(base):
        return [
            copy(
                small.at[base + 4], small.at[base + 4 + k], sm_s.at[base + 4 + k], sm_r.at[base + 4 + k],
                at(y_=rotate(y, k, NY)),
            )
            for k in (1, 2, 3)
        ]

    def reduce_y(base):
        copy(small.at[base + 2], small.at[base + 3], sm_s.at[base + 2], sm_r.at[base + 3], at(zl_=1 - zl)).wait()
        small[base + 4] = small[base + 2] + small[base + 3]
        for c in reduce_y_copies(base):
            c.start()

    def reduce_end(base):
        for c in reduce_y_copies(base):
            c.wait()
        return (small[base + 4] + small[base + 5]) + (small[base + 6] + small[base + 7])

    reduce_start(0, total_lanes(squares))

    cut = 9 * 16
    parts = (pl.ds(0, cut), pl.ds(cut, raw.shape[2] - cut))

    def s2_direct(half, up):
        to = at(y_=rotate(y, 1 if up else 3, NY))
        piece = raw.at[half, y]
        return copy(piece, piece, s2_s.at[half, int(up)], s2_r.at[half, int(up)], to)

    def s2_arrival(half, up):
        to = at(y_=rotate(y, 1 if up else 3, NY))
        piece = raw.at[half, rotate(y, 3 if up else 1, NY)]
        return copy(piece, piece, s2_s.at[half, int(up)], s2_r.at[half, int(up)], to)

    def s2_forward(half, up):
        to = at(y_=rotate(y, 1 if up else 3, NY))
        piece = raw.at[half, rotate(y, 3 if up else 1, NY), parts[0 if up else 1]]
        return copy(piece, piece, s2f_s.at[half, int(up)], s2f_r.at[half, int(up)], to)

    def s2_last(half, up):
        to = at(y_=rotate(y, 1 if up else 3, NY))
        piece = raw.at[half, rotate(y, 2, NY), parts[0 if up else 1]]
        return copy(piece, piece, s2f_s.at[half, int(up)], s2f_r.at[half, int(up)], to)

    def s3_copy(half, k):
        piece = a.at[core + 2 * half, rotate(y, 4 - k, NY)]
        return copy(piece, piece, s3_s.at[half, k], s3_r.at[half, k], at(core_=other))

    def s3_arrival(half, k):
        piece = a.at[other + 2 * half, rotate(y, 4 - k, NY)]
        return copy(piece, piece, s3_s.at[half, k], s3_r.at[half, k], at(core_=other))

    def normalise(half, k):
        s = rotate(y, 4 - k, NY)
        g = raw[half, s, rows : rows + 16, :].astype(F32)[:1]
        v = raw[half, s, :rows, :].astype(F32) * wide(piece_inv[half]) * g
        a[core + 2 * half, s] = v.astype(BF16)
        s3_copy(half, k).start()

    def wide(v):
        return jnp.concatenate([v] * (feats // 128), axis=1)

    def inverse(row):
        return 1.0 / jnp.sqrt(spread(row) / width + EPS)

    def xt_copy(k):
        return copy(xtot.at[x], xtot.at[x], xt_s.at[k - 1], xt_r.at[k - 1], at(x_=rotate(x, k, NX)))

    def xt_arrival(k):
        piece = xtot.at[rotate(x, 4 - k, NX)]
        return copy(piece, piece, xt_s.at[k - 1], xt_r.at[k - 1], at(x_=rotate(x, k, NX)))

    reduce_zl(0)
    s1_far.wait_send()
    w_send(0)
    reduce_y(0)
    for half in (0, 1):
        copy(ext, raw.at[half, y], s1_s.at[0], s1_r.at[half], at(core_=other)).wait_recv()
        for up in (True, False):
            s2_direct(half, up).start()
    w_send(1)
    xtot[x] = reduce_end(0)
    for k in (1, 2, 3):
        xt_copy(k).start()
    for half in (0, 1):
        for up in (True, False):
            s2_arrival(half, up).wait_recv()
            s2_forward(half, up).start()
    pump(0)
    w_send(2)
    for k in (1, 2, 3):
        xt_arrival(k).wait_recv()
    inv_ref[...] = inverse(xtot[x][:1])
    for half in (0, 1):
        piece_inv[half] = inverse(xtot[core + 2 * half][:1])
    racc[...] = jnp.zeros_like(racc)
    for half in (0, 1):
        for k in (0, 1, 3):
            normalise(half, k)
    pump(1)
    w_send(3)
    for half in (0, 1):
        for up in (True, False):
            s2_last(half, up).wait_recv()
        normalise(half, 2)
    load_q.wait()
    load_og.wait()
    pltpu.make_async_copy(wg.at[0], wg.at[0], local_sem.at[3]).wait()
    for half in (0, 1):
        for k in (0, 1, 3, 2):
            s3_arrival(half, k).wait_recv()

    def sequence(b):
        return pl.ds(pl.multiple_of(b * src, src), src)

    def rs_copy(c, j, b):
        part = sequence(b)
        return copy(
            part_send.at[c, j, part], rs_recv.at[c, j, part], rs_s.at[c, j, b], rs_r.at[c, j, b],
            at(x_=rotate(x, 1 + j, NX)),
        )

    def ag_copy(c, j, b):
        piece = ag.at[c, x, sequence(b)]
        return copy(piece, piece, ag_s.at[c, j, b], ag_r.at[c, j, b], at(x_=rotate(x, 1 + j, NX)))

    def ag_arrival(c, j, b):
        piece = ag.at[c, rotate(x, 3 - j, NX), sequence(b)]
        return copy(piece, piece, ag_s.at[c, j, b], ag_r.at[c, j, b], at(x_=rotate(x, 1 + j, NX)))

    def project(c):
        for up in (True, False):
            w_forward(c, up).wait_recv()

        def one(j):
            xs = rotate(x, 1 + j, NX)
            acc = jnp.zeros((rows, cols), F32)
            for r in range(4):
                acc = acc + jnp.dot(a[xs, rotate(zh, r, NZ)], wg[r, c], preferred_element_type=F32)
            return acc

        def send(j, carry):
            part_send[c, j] = one(j).astype(BF16)
            for b in range(batches):
                rs_copy(c, j, b).start()
            return carry

        lax.fori_loop(0, 3, send, 0)
        own_part[c] = one(3)

    lane = lax.broadcasted_iota(jnp.int32, (1, 128), 1)
    first = lane < HEAD_DIM
    place = lax.rem(lax.broadcasted_iota(jnp.int32, (1, 2 * src), 1), src)

    def two_heads(v):
        return jnp.concatenate([jnp.where(first, v, 0.0), jnp.where(first, 0.0, v)], axis=0).astype(BF16)

    def per_head(v, f):
        return jnp.concatenate([f(v[:, :src]), f(v[:, src:])], axis=1)

    def dot_t(m, n):
        return lax.dot_general(m, n, (((1,), (1,)), ((), ())), preferred_element_type=F32)

    def t_dot(m, n):
        return lax.dot_general(m, n, (((0,), (0,)), ((), ())), preferred_element_type=F32)

    def attend(c):
        lanes = pl.ds(pl.multiple_of(c * 128, 128), 128)

        def one(b, carry):
            at_rows = sequence(b)
            kv_b = own_part[c, at_rows, :]
            for j in range(3):
                rs_copy(c, j, b).wait_recv()
                kv_b = kv_b + rs_recv[c, j, at_rows, :].astype(F32)
            keys = two_heads(kv_b[:, :128].astype(BF16).astype(F32))
            values = two_heads(kv_b[:, 128:].astype(BF16).astype(F32))
            query, cotan = q_ref[b, :, lanes], og_ref[b, :, lanes]
            expo = jnp.where(place < len_ref[b], jnp.exp(dot_t(query, keys) * SCALE), 0.0)
            probs = per_head(expo, lambda e: e / jnp.sum(e, axis=-1, keepdims=True))
            probs_b = probs.astype(BF16)
            att_ref[b, :, lanes] = jnp.dot(probs_b, values, preferred_element_type=F32).astype(BF16)
            dprob = dot_t(cotan, values)
            delta = per_head(
                probs * dprob, lambda e: jnp.broadcast_to(jnp.sum(e, axis=-1, keepdims=True), e.shape)
            )
            dscore = (probs * (dprob - delta) * SCALE).astype(BF16)
            gq_ref[b, :, lanes] = jnp.dot(dscore, keys, preferred_element_type=F32).astype(BF16)
            dkey, dvalue = t_dot(dscore, query), t_dot(probs_b, cotan)
            dkv = jnp.concatenate(
                [jnp.where(first, dkey[:src], dkey[src:]), jnp.where(first, dvalue[:src], dvalue[src:])], axis=1
            ).astype(BF16)
            ag[c, x, at_rows, :] = dkv
            for j in range(3):
                ag_copy(c, j, b).start()
            product = dkv.astype(F32) * kv_b
            racc[at_rows, :] = racc[at_rows, :] + (product[:, :128] + product[:, 128:])
            return carry

        lax.fori_loop(0, batches, one, 0)

    def back(chunks):
        for c in chunks:
            for j in range(3):
                for b in range(batches):
                    ag_arrival(c, j, b).wait_recv()

        def one(i, carry):
            xs, r = i // 4, lax.rem(i, 4)
            term = dot_t(ag[chunks[0], xs], wg[r, chunks[0]])
            for c in chunks[1:]:
                term = term + dot_t(ag[c, xs], wg[r, c])
            dn[xs, r] = term if chunks[0] == 0 else dn[xs, r] + term
            return carry

        lax.fori_loop(0, 16, one, 0)

    project(0)
    pump(2)
    attend(0)
    project(1)
    attend(1)
    pump(3)
    project(2)
    back((0, 1))
    attend(2)
    project(3)
    attend(3)
    reduce_start(8, total_lanes(racc[...]))
    back((2,))
    reduce_zl(8)
    last = CHUNKS - 1

    def d1_copy(b, half, k):
        part = sequence(b)
        return copy(
            core_send.at[half, k, part], core_recv.at[half, k, part],
            d1_s.at[b, half, k], d1_r.at[b, half, k], at(core_=other),
        )

    def d2_copy(b, half, k):
        part = sequence(b)
        return copy(
            y_send.at[half, k - 1, part], y_recv.at[half, k - 1, part],
            d2_s.at[b, half, k - 1], d2_r.at[b, half, k - 1], at(y_=rotate(y, k, NY)),
        )

    def whole(b, xs, k):
        part = sequence(b)
        r = lax.rem(y + k + NZ - zh, NZ)
        return dn[xs, r, part, :] + dot_t(ag[last, xs, part, :], wg[r, last])

    def dz_copy(b):
        part = sequence(b)
        return copy(z_send.at[part], z_recv.at[part], dz_s.at[b], dz_r.at[b], at(zl_=1 - zl))

    def chip_sum(b, half, k):
        v = whole(b, core + 2 * half, k)
        d1_copy(b, half, k).wait_recv()
        return v + core_recv[half, k, sequence(b), :].astype(F32)

    for b in range(batches):
        part = sequence(b)
        for j in range(3):
            ag_arrival(last, j, b).wait_recv()
        for k in (2, 1, 3, 0):
            for half in (0, 1):
                core_send[half, k, part, :] = whole(b, other + 2 * half, k).astype(BF16)
                d1_copy(b, half, k).start()
        if b == 0:
            reduce_y(8)
        z_send[part, :] = chip_sum(b, 1 - zl, 2).astype(BF16)
        dz_copy(b).start()
        for half in (0, 1):
            for k in (1, 3):
                y_send[half, k - 1, part, :] = chip_sum(b, half, k).astype(BF16)
                d2_copy(b, half, k).start()
        v = chip_sum(b, zl, 2)
        dz_copy(b).wait_recv()
        y_send[0, 1, part, :] = (v + z_recv[part, :].astype(F32)).astype(BF16)
        d2_copy(b, 0, 2).start()
        for half in (0, 1):
            y_own[half, part, :] = chip_sum(b, half, 0)
    inv = inv_ref[...]
    rsum_ref[...] = spread(reduce_end(8)[:1]) * inv * inv / width

    def d3_copy(b, half):
        part = pl.ds(b * src, src)
        to = (y, zh * 4 + core + 2 * half, x)
        return copy(fin_send.at[half, part], fin.at[zl, part], d3_s.at[b, half], d3_r.at[b, zl], to)

    def stays(half):
        return jnp.logical_and(home, x // 2 == half)

    gain_sum = jnp.zeros((1, feats), F32)
    for b in range(batches):
        part = pl.ds(b * src, src)
        for half in (0, 1):
            v = y_own[half, part, :]
            for k in (1, 3):
                d2_copy(b, half, k).wait_recv()
                v = v + y_recv[half, k - 1, part, :].astype(F32)
            if half == 0:
                d2_copy(b, 0, 2).wait_recv()
            v = v + jnp.where(zl == half, y_recv[0, 1, part, :].astype(F32), 0.0)
            fin_send[half, part, :] = v.astype(BF16)

            @pl.when(stays(half))
            def _():
                pltpu.make_async_copy(fin_send.at[half, part], fin.at[zl, part], d3_r.at[b, zl]).start()

            @pl.when(jnp.logical_not(stays(half)))
            def _():
                d3_copy(b, half).start()

            hidden = raw[half, y, part, :].astype(F32) * wide(piece_inv[half, part, :])
            gain_sum = gain_sum + jnp.sum(v * hidden, axis=0, keepdims=True)

    def gz_copy(k):
        return copy(gz.at[zh], gz.at[zh], gz_s.at[k - 1], gz_r.at[k - 1], at(zh_=rotate(zh, k, NZ)))

    def gz_arrival(k):
        piece = gz.at[rotate(zh, 4 - k, NZ)]
        return copy(piece, piece, gz_s.at[k - 1], gz_r.at[k - 1], at(zh_=rotate(zh, k, NZ)))

    def gx_copy(x_):
        place = 2 * zl + core
        return copy(gz.at[4], gx.at[place], gx_s.at[x_], gx_r.at[place], (y, zh * 4 + x_, x))

    gz[zh] = jnp.broadcast_to(gain_sum, (8, feats))
    for k in (1, 2, 3):
        gz_copy(k).start()

    def owned(b):
        part = pl.ds(b * src, src)
        for k in (0, 1):
            copy(fin_send.at[0, part], fin.at[k, part], d3_s.at[b, 0], d3_r.at[b, k], at(core_=other)).wait_recv()
        dnormed = fin[0, part, :].astype(F32) + fin[1, part, :].astype(F32)
        own_gain = ext[rows : rows + 16, :].astype(F32)[:1]
        gs_ref[part, :] = own_gain * (wide(inv_ref[part, :]) * dnormed) - ext[part, :].astype(F32) * wide(
            rsum_ref[part, :]
        )

    owned(0)
    for k in (1, 2, 3):
        gz_arrival(k).wait_recv()
    gz[4] = (gz[0] + gz[1]) + (gz[2] + gz[3])
    for x_ in range(NX):
        itself = jnp.logical_and(home, x == x_)

        @pl.when(itself)
        def _():
            place = 2 * zl + core
            pltpu.make_async_copy(gz.at[4], gx.at[place], gx_r.at[place]).start()

        @pl.when(jnp.logical_not(itself))
        def _():
            gx_copy(x_).start()

    owned(1)

    def sent_w(c, carry):
        for up in (True, False):
            w_direct(c, up).wait_send()
            w_forward(c, up).wait_send()
        for j in range(3):
            for b in range(batches):
                rs_copy(c, j, b).wait_send()
                ag_copy(c, j, b).wait_send()
        return carry

    lax.fori_loop(0, CHUNKS, sent_w, 0)

    @pl.when(jnp.logical_not(home))
    def _():
        s1_near.wait_send()

    for half in (0, 1):
        for up in (True, False):
            s2_direct(half, up).wait_send()
            s2_forward(half, up).wait_send()
        for k in range(4):
            s3_copy(half, k).wait_send()
        for b in range(batches):
            for k in range(4):
                d1_copy(b, half, k).wait_send()
            for k in (1, 3) if half else (1, 2, 3):
                d2_copy(b, half, k).wait_send()
            if half == 0:
                dz_copy(b).wait_send()

            @pl.when(jnp.logical_not(stays(half)))
            def _():
                d3_copy(b, half).wait_send()

    for k in (1, 2, 3):
        xt_copy(k).wait_send()
        gz_copy(k).wait_send()
    for x_ in range(NX):

        @pl.when(jnp.logical_not(jnp.logical_and(home, x == x_)))
        def _():
            gx_copy(x_).wait_send()

    for k in range(4):
        copy(gz.at[4], gx.at[k], gx_s.at[0], gx_r.at[k], at(core_=other)).wait_recv()
    gg_ref[...] = ((gx[0] + gx[1]) + (gx[2] + gx[3]))[:1]


def per_device(states, gain, kv_weight, queries, out_grad, src_len):
    batches, src, feats = states.shape
    tgt, heads_cols = queries.shape[2:]
    rows = batches * src
    cols = 2 * heads_cols // CHUNKS
    w = kv_weight.reshape(feats, 2 * heads_cols)
    ext = jnp.concatenate([states.reshape(rows, feats), jnp.broadcast_to(gain[None, :], (16, feats))], axis=0)
    vmem = pl.BlockSpec(memory_space=pltpu.VMEM)
    dma = pltpu.SemaphoreType.DMA
    out = pl.pallas_call(
        kernel,
        out_shape=(
            jax.ShapeDtypeStruct((batches, tgt, heads_cols), BF16),
            jax.ShapeDtypeStruct((batches, tgt, heads_cols), BF16),
            jax.ShapeDtypeStruct((rows, feats), F32),
            jax.ShapeDtypeStruct((1, feats), F32),
        ),
        in_specs=[pl.BlockSpec(memory_space=pl.ANY)] * 4 + [pl.BlockSpec(memory_space=pltpu.SMEM)],
        out_specs=[vmem] * 4,
        scratch_shapes=[
            pltpu.VMEM((rows + 16, feats), BF16),
            pltpu.VMEM((batches, tgt, heads_cols), BF16),
            pltpu.VMEM((batches, tgt, heads_cols), BF16),
            pltpu.VMEM((4, CHUNKS, feats, cols), BF16),
            pltpu.VMEM((2, 4, rows + 16, feats), BF16),
            pltpu.VMEM((4, 4, rows, feats), BF16),
            pltpu.VMEM((CHUNKS, rows, cols), F32),
            pltpu.VMEM((CHUNKS, 3, rows, cols), BF16),
            pltpu.VMEM((CHUNKS, 3, rows, cols), BF16),
            pltpu.VMEM((CHUNKS, 4, rows, cols), BF16),
            pltpu.VMEM((4, 4, rows, feats), F32),
            pltpu.VMEM((2, 4, rows, feats), BF16),
            pltpu.VMEM((2, 4, rows, feats), BF16),
            pltpu.VMEM((rows, feats), BF16),
            pltpu.VMEM((rows, feats), BF16),
            pltpu.VMEM((2, 3, rows, feats), BF16),
            pltpu.VMEM((2, 3, rows, feats), BF16),
            pltpu.VMEM((2, rows, feats), F32),
            pltpu.VMEM((2, rows, feats), BF16),
            pltpu.VMEM((2, rows, feats), BF16),
            pltpu.VMEM((rows, 128), F32),
            pltpu.VMEM((16, 8, rows), F32),
            pltpu.VMEM((4, 8, rows), F32),
            pltpu.VMEM((5, 8, feats), F32),
            pltpu.VMEM((4, 8, feats), F32),
            pltpu.VMEM((rows, 128), F32),
            pltpu.VMEM((2, rows, 128), F32),
            pltpu.VMEM((rows, 128), F32),
            dma((4,)),
            dma((2, CHUNKS)), dma((2, CHUNKS)), dma((2, CHUNKS)), dma((2, CHUNKS)),
            dma((2,)), dma((2,)),
            dma((2, 2)), dma((2, 2)), dma((2, 2)), dma((2, 2)),
            dma((2, 4)), dma((2, 4)),
            dma((CHUNKS, 3, 2)), dma((CHUNKS, 3, 2)),
            dma((CHUNKS, 3, 2)), dma((CHUNKS, 3, 2)),
            dma((2, 2, 4)), dma((2, 2, 4)),
            dma((2,)), dma((2,)),
            dma((2, 2, 3)), dma((2, 2, 3)),
            dma((2, 2)), dma((2, 2)),
            dma((16,)), dma((16,)),
            dma((3,)), dma((3,)),
            dma((3,)), dma((3,)),
            dma((4,)), dma((4,)),
        ],
        compiler_params=pltpu.CompilerParams(
            collective_id=1, has_side_effects=True, vmem_limit_bytes=52 * 2**20
        ),
        name="cross_attention",
    )(
        w, ext, queries[0], out_grad[0], src_len
    )
    attended, grad_q, grad_states, grad_gain = out
    return attended[None], grad_q[None], grad_states.reshape(batches, src, feats), grad_gain[0]


def solution(mesh):
    return jax.shard_map(
        per_device,
        mesh=mesh,
        in_specs=(
            P("dp", None, ("section", "tensor")),
            P(("section", "tensor")),
            P("section", "dp", None, "tensor"),
            P("section", "dp", None, "tensor"),
            P("section", "dp", None, "tensor"),
            P("dp"),
        ),
        out_specs=(
            P("section", "dp", None, "tensor"),
            P("section", "dp", None, "tensor"),
            P("dp", None, ("section", "tensor")),
            P(("section", "tensor")),
        ),
        check_vma=False,
    )
```

```python
import jax
import jax.numpy as jnp
from jax import lax
from jax.experimental import pallas as pl
from jax.experimental.pallas import tpu as pltpu
from jax.sharding import PartitionSpec as P

MESH = pl.DeviceIdType.MESH
HEAD_DIM = 64
SCALE = HEAD_DIM ** (-0.5)
EPS = 1e-06
NX, NY, NZ = 4, 4, 4
CHUNKS = 4
F32, BF16 = jnp.float32, jnp.bfloat16


def rotate(a, by, n):
    return lax.rem(a + by, n)


def kernel(
    w_ref, ext_ref, q_in, og_in, len_ref,
    att_ref, gq_ref, gs_ref, gg_ref,
    ext, q_ref, og_ref, wg, through, through_half, turned, raw, a, own_part, part_send, rs_recv, ag, dn, core_send, core_recv, z_send, z_recv, y_send, y_recv,
    y_own, fin_send, fin, racc, small, xtot, gz, gy, gx, inv_ref, piece_inv, rsum_ref,
    local_sem, w_s, w_r, s1_s, s1_r, s2_s, s2_r, s2f_s, s2f_r, s3_s, s3_r, rs_s, rs_r, ag_s, ag_r,
    d1_s, d1_r, dz_s, dz_r, d2_s, d2_r, d3_s, d3_r, sm_s, sm_r, xt_s, xt_r, gz_s, gz_r, gy_s, gy_r, gx_s, gx_r,
):
    y, d, t = lax.axis_index("section"), lax.axis_index("dp"), lax.axis_index("tensor")
    zh, x, zl, core = d // 4, lax.rem(d, 4), t // 2, lax.rem(t, 2)
    rows, feats = gs_ref.shape
    batches = q_ref.shape[0]
    src = rows // batches
    cols = wg.shape[3]
    heads_cols = q_ref.shape[2]
    width = NX * NZ * feats

    def at(y_=None, zh_=None, x_=None, zl_=None, core_=None):
        pick = lambda new, old: old if new is None else new
        return (pick(y_, y), pick(zh_, zh) * 4 + pick(x_, x), pick(zl_, zl) * 2 + pick(core_, core))

    def copy(src_ref, dst_ref, send, recv, to):
        return pltpu.make_async_remote_copy(
            src_ref=src_ref, dst_ref=dst_ref, send_sem=send, recv_sem=recv, device_id=to, device_id_type=MESH
        )

    other = 1 - core
    home = t == x

    load_ext = pltpu.make_async_copy(ext_ref, ext, local_sem.at[0])
    load_q = pltpu.make_async_copy(q_in, q_ref, local_sem.at[1])
    load_og = pltpu.make_async_copy(og_in, og_ref, local_sem.at[2])
    load_ext.start()
    load_q.start()
    load_og.start()
    barrier = pltpu.get_barrier_semaphore()

    def greet(to):
        pl.semaphore_signal(barrier, inc=1, device_id=to, device_id_type=MESH)

    for k in (1, 2, 3):
        greet(at(zh_=rotate(zh, k, NZ)))
        greet(at(y_=rotate(y, k, NY)))
        greet(at(x_=rotate(x, k, NX)))
    greet(at(core_=other))
    above = at(zh_=rotate(zh, zl, NZ), zl_=1 - zl)
    below = at(zh_=rotate(zh, 3 + zl, NZ), zl_=1 - zl)
    greet(above)
    greet(below)
    for zl_ in (0, 1):
        for core_ in (0, 1):
            itself = jnp.logical_and(home, jnp.logical_and(zl == zl_, core == core_))

            @pl.when(jnp.logical_not(itself))
            def _():
                greet(at(x_=t, zl_=zl_, core_=core_))

    for x_ in range(NX):

        @pl.when(jnp.logical_not(jnp.logical_and(home, x == x_)))
        def _():
            greet((y, zh * 4 + x_, x))

    @pl.when(jnp.logical_not(home))
    def _():
        pl.semaphore_wait(barrier, 20)

    @pl.when(home)
    def _():
        pl.semaphore_wait(barrier, 18)

    x_core = lax.rem(x, 2)

    def w_lanes(c):
        k = pl.ds(pl.multiple_of(c * 128, 128), 128)
        v = pl.ds(pl.multiple_of(heads_cols + c * 128, 128), 128)
        return ((k, pl.ds(0, 128)), (v, pl.ds(128, 128)))

    def w_copy(stage, c, up):
        half = feats // 2
        part, rest = pl.ds(0 if up else half, half), pl.ds(half if up else 0, half)
        way, direct = int(up), wg.at[3 if up else 1, c]
        here, there = (
            (through.at[way, c], through.at[way, c]),
            (through.at[way, c, part], direct.at[part]),
            (direct.at[part], through_half.at[way, c]),
            (through_half.at[way, c], wg.at[2, c, part]),
            (through.at[way, c, rest], direct.at[rest]),
        )[stage]
        return copy(here, there, w_s.at[stage, way, c], w_r.at[stage, way, c], above if up else below)

    def w_send(c):
        for up in (True, False):
            for here, there in w_lanes(c):
                copy(
                    w_ref.at[:, here], through.at[int(up), c, :, there],
                    w_s.at[0, int(up), c], w_r.at[0, int(up), c], above if up else below,
                ).start()

    def hop(stage, c):
        for up in (True, False):
            w_copy(stage, c, up).wait_recv()
            w_copy(stage + 1, c, up).start()
            if stage == 0:
                w_copy(4, c, up).start()

    load_ext.wait()

    def s1_copy(z, to):
        return copy(ext, raw.at[x // 2, y], s1_s.at[z], s1_r.at[x // 2], to)

    s1_far = s1_copy(1, at(x_=t, zl_=1 - zl, core_=x_core))
    s1_near = s1_copy(0, at(x_=t, core_=x_core))
    s1_local = pltpu.make_async_copy(ext, raw.at[x // 2, y], s1_r.at[x // 2])
    s1_far.start()

    @pl.when(jnp.logical_not(home))
    def _():
        s1_near.start()

    @pl.when(home)
    def _():
        s1_local.start()

    for c in range(CHUNKS):
        for here, there in w_lanes(c):
            pltpu.make_async_copy(w_ref.at[:, here], wg.at[0, c, :, there], local_sem.at[3]).start()

    h = ext[:rows, :].astype(F32)
    squares = h * h

    def total_lanes(v):
        acc = v[:, :128]
        for k in range(128, v.shape[1], 128):
            acc = acc + v[:, k : k + 128]
        return jnp.broadcast_to(jnp.sum(acc.T, axis=0, keepdims=True), (8, rows))

    def spread(row):
        return jnp.broadcast_to(row, (128, rows)).T

    def reduce_start(base, v):
        small[base] = v
        c = copy(small.at[base], small.at[base + 1], sm_s.at[base], sm_r.at[base + 1], at(core_=other))
        c.start()

    def reduce_zl(base):
        copy(small.at[base], small.at[base + 1], sm_s.at[base], sm_r.at[base + 1], at(core_=other)).wait()
        small[base + 2] = small[base] + small[base + 1]
        copy(small.at[base + 2], small.at[base + 3], sm_s.at[base + 2], sm_r.at[base + 3], at(zl_=1 - zl)).start()

    def reduce_y_copies(base):
        return [
            copy(
                small.at[base + 4], small.at[base + 4 + k], sm_s.at[base + 4 + k], sm_r.at[base + 4 + k],
                at(y_=rotate(y, k, NY)),
            )
            for k in (1, 2, 3)
        ]

    def reduce_y(base):
        copy(small.at[base + 2], small.at[base + 3], sm_s.at[base + 2], sm_r.at[base + 3], at(zl_=1 - zl)).wait()
        small[base + 4] = small[base + 2] + small[base + 3]
        for c in reduce_y_copies(base):
            c.start()

    def reduce_end(base):
        for c in reduce_y_copies(base):
            c.wait()
        return (small[base + 4] + small[base + 5]) + (small[base + 6] + small[base + 7])

    reduce_start(0, total_lanes(squares))

    cut = 9 * 16
    parts = (pl.ds(0, cut), pl.ds(cut, raw.shape[2] - cut))

    def s2_direct(half, up):
        to = at(y_=rotate(y, 1 if up else 3, NY))
        piece = raw.at[half, y]
        return copy(piece, piece, s2_s.at[half, int(up)], s2_r.at[half, int(up)], to)

    def s2_arrival(half, up):
        to = at(y_=rotate(y, 1 if up else 3, NY))
        piece = raw.at[half, rotate(y, 3 if up else 1, NY)]
        return copy(piece, piece, s2_s.at[half, int(up)], s2_r.at[half, int(up)], to)

    def s2_forward(half, up):
        to = at(y_=rotate(y, 1 if up else 3, NY))
        piece = raw.at[half, rotate(y, 3 if up else 1, NY), parts[0 if up else 1]]
        return copy(piece, piece, s2f_s.at[half, int(up)], s2f_r.at[half, int(up)], to)

    def s2_last(half, up):
        to = at(y_=rotate(y, 1 if up else 3, NY))
        piece = raw.at[half, rotate(y, 2, NY), parts[0 if up else 1]]
        return copy(piece, piece, s2f_s.at[half, int(up)], s2f_r.at[half, int(up)], to)

    def s3_copy(half, k):
        piece = a.at[core + 2 * half, rotate(y, 4 - k, NY)]
        return copy(piece, piece, s3_s.at[half, k], s3_r.at[half, k], at(core_=other))

    def s3_arrival(half, k):
        piece = a.at[other + 2 * half, rotate(y, 4 - k, NY)]
        return copy(piece, piece, s3_s.at[half, k], s3_r.at[half, k], at(core_=other))

    def normalise(half, k):
        s = rotate(y, 4 - k, NY)
        g = raw[half, s, rows : rows + 16, :].astype(F32)[:1]
        v = raw[half, s, :rows, :].astype(F32) * wide(piece_inv[half]) * g
        a[core + 2 * half, s] = v.astype(BF16)
        s3_copy(half, k).start()

    def wide(v):
        return jnp.concatenate([v] * (feats // 128), axis=1)

    def inverse(row):
        return 1.0 / jnp.sqrt(spread(row) / width + EPS)

    def xt_copy(k):
        return copy(xtot.at[x], xtot.at[x], xt_s.at[k - 1], xt_r.at[k - 1], at(x_=rotate(x, k, NX)))

    def xt_arrival(k):
        piece = xtot.at[rotate(x, 4 - k, NX)]
        return copy(piece, piece, xt_s.at[k - 1], xt_r.at[k - 1], at(x_=rotate(x, k, NX)))

    reduce_zl(0)
    s1_far.wait_send()
    w_send(0)
    reduce_y(0)
    for half in (0, 1):
        copy(ext, raw.at[half, y], s1_s.at[0], s1_r.at[half], at(core_=other)).wait_recv()
        for up in (True, False):
            s2_direct(half, up).start()
    w_send(1)
    xtot[x] = reduce_end(0)
    for k in (1, 2, 3):
        xt_copy(k).start()
    hop(0, 0)
    for k in (1, 2, 3):
        xt_arrival(k).wait_recv()
    inv_ref[...] = inverse(xtot[x][:1])
    for half in (0, 1):
        piece_inv[half] = inverse(xtot[core + 2 * half][:1])
    racc[...] = jnp.zeros_like(racc)
    for half in (0, 1):
        normalise(half, 0)
    hop(0, 1)
    for half in (0, 1):
        for up in (True, False):
            s2_arrival(half, up).wait_recv()
            s2_forward(half, up).start()
    hop(1, 0)
    w_send(2)
    for half in (0, 1):
        for k in (1, 3):
            normalise(half, k)
    hop(1, 1)
    for half in (0, 1):
        for up in (True, False):
            s2_last(half, up).wait_recv()
        normalise(half, 2)
    hop(2, 0)
    load_q.wait()
    load_og.wait()
    pltpu.make_async_copy(wg.at[0], wg.at[0], local_sem.at[3]).wait()
    for half in (0, 1):
        for k in (0, 1, 3, 2):
            s3_arrival(half, k).wait_recv()
    hop(0, 2)
    hop(2, 1)

    def sequence(b):
        return pl.ds(pl.multiple_of(b * src, src), src)

    def rs_copy(c, j, b):
        part = sequence(b)
        return copy(
            part_send.at[c, j, part], rs_recv.at[c, j, part], rs_s.at[c, j, b], rs_r.at[c, j, b],
            at(x_=rotate(x, 1 + j, NX)),
        )

    def ag_copy(c, j, b):
        piece = ag.at[c, x, sequence(b)]
        return copy(piece, piece, ag_s.at[c, j, b], ag_r.at[c, j, b], at(x_=rotate(x, 1 + j, NX)))

    def ag_arrival(c, j, b):
        piece = ag.at[c, rotate(x, 3 - j, NX), sequence(b)]
        return copy(piece, piece, ag_s.at[c, j, b], ag_r.at[c, j, b], at(x_=rotate(x, 1 + j, NX)))

    def project(c):
        for up in (True, False):
            w_copy(4, c, up).wait_recv()
            w_copy(3, c, up).wait_recv()

        def one(j, b):
            xs = rotate(x, 1 + j, NX)
            acc = jnp.zeros((src, cols), F32)
            for r in range(4):
                acc = acc + jnp.dot(a[xs, rotate(zh, r, NZ), sequence(b), :], wg[r, c], preferred_element_type=F32)
            return acc

        def sequences(b, carry):
            for j in range(3):
                part_send[c, j, sequence(b), :] = one(j, b).astype(BF16)
                rs_copy(c, j, b).start()
            own_part[c, sequence(b), :] = one(3, b)
            return carry

        lax.fori_loop(0, batches, sequences, 0)

    lane = lax.broadcasted_iota(jnp.int32, (1, 128), 1)
    first = lane < HEAD_DIM
    place = lax.rem(lax.broadcasted_iota(jnp.int32, (1, 2 * src), 1), src)

    def two_heads(v):
        return jnp.concatenate([jnp.where(first, v, 0.0), jnp.where(first, 0.0, v)], axis=0).astype(BF16)

    def per_head(v, f):
        return jnp.concatenate([f(v[:, :src]), f(v[:, src:])], axis=1)

    def dot_t(m, n):
        return lax.dot_general(m, n, (((1,), (1,)), ((), ())), preferred_element_type=F32)

    def t_dot(m, n):
        return lax.dot_general(m, n, (((0,), (0,)), ((), ())), preferred_element_type=F32)

    def attend(c):
        lanes = pl.ds(pl.multiple_of(c * 128, 128), 128)

        def one(b, carry):
            at_rows = sequence(b)
            kv_b = own_part[c, at_rows, :]
            for j in range(3):
                rs_copy(c, j, b).wait_recv()
                kv_b = kv_b + rs_recv[c, j, at_rows, :].astype(F32)
            keys = two_heads(kv_b[:, :128].astype(BF16).astype(F32))
            values = two_heads(kv_b[:, 128:].astype(BF16).astype(F32))
            query, cotan = q_ref[b, :, lanes], og_ref[b, :, lanes]
            expo = jnp.where(place < len_ref[b], jnp.exp(dot_t(query, keys) * SCALE), 0.0)
            probs = per_head(expo, lambda e: e / jnp.sum(e, axis=-1, keepdims=True))
            probs_b = probs.astype(BF16)
            att_ref[b, :, lanes] = jnp.dot(probs_b, values, preferred_element_type=F32).astype(BF16)
            dprob = dot_t(cotan, values)
            delta = per_head(
                probs * dprob, lambda e: jnp.broadcast_to(jnp.sum(e, axis=-1, keepdims=True), e.shape)
            )
            dscore = (probs * (dprob - delta) * SCALE).astype(BF16)
            gq_ref[b, :, lanes] = jnp.dot(dscore, keys, preferred_element_type=F32).astype(BF16)
            dkey, dvalue = t_dot(dscore, query), t_dot(probs_b, cotan)
            dkv = jnp.concatenate(
                [jnp.where(first, dkey[:src], dkey[src:]), jnp.where(first, dvalue[:src], dvalue[src:])], axis=1
            ).astype(BF16)
            ag[c, x, at_rows, :] = dkv
            for j in range(3):
                ag_copy(c, j, b).start()
            product = dkv.astype(F32) * kv_b
            racc[at_rows, :] = racc[at_rows, :] + (product[:, :128] + product[:, 128:])
            return carry

        lax.fori_loop(0, batches, one, 0)

    def back(chunks):
        for c in chunks:
            for j in range(3):
                for b in range(batches):
                    ag_arrival(c, j, b).wait_recv()

        def one(r, carry):
            term = dot_t(ag[chunks[0]].reshape(4 * rows, cols), wg[r, chunks[0]])
            for c in chunks[1:]:
                term = term + dot_t(ag[c].reshape(4 * rows, cols), wg[r, c])
            for xs in range(4):
                mine = term[xs * rows : (xs + 1) * rows]
                dn[xs, r] = mine if chunks[0] == 0 else dn[xs, r] + mine
            return carry

        lax.fori_loop(0, 4, one, 0)

    project(0)
    hop(1, 2)
    w_send(3)
    project(1)
    attend(0)
    hop(2, 2)
    attend(1)
    hop(0, 3)
    back((0,))
    project(2)
    hop(1, 3)
    back((1,))
    hop(2, 3)
    attend(2)
    project(3)
    attend(3)
    reduce_start(8, total_lanes(racc[...]))
    last = CHUNKS - 1
    for r in range(4):
        turned[r] = wg[r, last].T
    back((2,))
    reduce_zl(8)

    def d1_copy(b, half, k):
        part = sequence(b)
        return copy(
            core_send.at[half, k, part], core_recv.at[half, k, part],
            d1_s.at[b, half, k], d1_r.at[b, half, k], at(core_=other),
        )

    def d2_copy(b, half, k):
        part = sequence(b)
        return copy(
            y_send.at[half, k - 1, part], y_recv.at[half, k - 1, part],
            d2_s.at[b, half, k - 1], d2_r.at[b, half, k - 1], at(y_=rotate(y, k, NY)),
        )

    def whole(b, xs, k):
        part = sequence(b)
        r = lax.rem(y + k + NZ - zh, NZ)
        return dn[xs, r, part, :] + jnp.dot(ag[last, xs, part, :], turned[r], preferred_element_type=F32)

    def dz_copy(b):
        part = sequence(b)
        return copy(z_send.at[part], z_recv.at[part], dz_s.at[b], dz_r.at[b], at(zl_=1 - zl))

    def chip_sum(b, half, k):
        v = whole(b, core + 2 * half, k)
        d1_copy(b, half, k).wait_recv()
        return v + core_recv[half, k, sequence(b), :].astype(F32)

    def cores(b):
        for j in range(3):
            ag_arrival(last, j, b).wait_recv()
        part = sequence(b)
        for k in (2, 1, 3, 0):
            for half in (0, 1):
                core_send[half, k, part, :] = whole(b, other + 2 * half, k).astype(BF16)
                d1_copy(b, half, k).start()
        if b == 0:
            reduce_y(8)
        z_send[part, :] = chip_sum(b, 1 - zl, 2).astype(BF16)
        dz_copy(b).start()

    def one_step(b):
        for half in (0, 1):
            for k in (1, 3):
                y_send[half, k - 1, sequence(b), :] = chip_sum(b, half, k).astype(BF16)
                d2_copy(b, half, k).start()

    def two_steps(b):
        part = sequence(b)
        v = chip_sum(b, zl, 2)
        dz_copy(b).wait_recv()
        y_send[0, 1, part, :] = (v + z_recv[part, :].astype(F32)).astype(BF16)
        d2_copy(b, 0, 2).start()

    cores(0)
    one_step(0)
    cores(1)
    two_steps(0)
    one_step(1)
    two_steps(1)
    for b in range(batches):
        for half in (0, 1):
            y_own[half, sequence(b), :] = chip_sum(b, half, 0)

    def d3_copy(b, half):
        part = pl.ds(b * src, src)
        to = (y, zh * 4 + core + 2 * half, x)
        return copy(fin_send.at[half, part], fin.at[zl, part], d3_s.at[b, half], d3_r.at[b, zl], to)

    def stays(half):
        return jnp.logical_and(home, x // 2 == half)

    def deliver(b):
        part = pl.ds(b * src, src)
        for k in (1, 3):
            for half in (0, 1):
                d2_copy(b, half, k).wait_recv()
        d2_copy(b, 0, 2).wait_recv()
        for half in (0, 1):
            v = y_own[half, part, :]
            for k in (1, 3):
                v = v + y_recv[half, k - 1, part, :].astype(F32)
            v = v + jnp.where(zl == half, y_recv[0, 1, part, :].astype(F32), 0.0)
            fin_send[half, part, :] = v.astype(BF16)

            @pl.when(stays(half))
            def _():
                pltpu.make_async_copy(fin_send.at[half, part], fin.at[zl, part], d3_r.at[b, zl]).start()

            @pl.when(jnp.logical_not(stays(half)))
            def _():
                d3_copy(b, half).start()

    def weighed(v, half, k):
        hidden = raw[half, rotate(y, k, NY), :rows, :].astype(F32) * wide(piece_inv[half])
        return jnp.sum(v.astype(F32) * hidden, axis=0, keepdims=True)

    def folded(v):
        lanes = [v[:, i : i + 128] for i in range(0, feats, 128)]
        return jnp.concatenate(lanes + lanes, axis=0)

    def gz_copy(k):
        return copy(gz.at[zh], gz.at[zh], gz_s.at[k - 1], gz_r.at[k - 1], at(zh_=rotate(zh, k, NZ)))

    def gz_arrival(k):
        piece = gz.at[rotate(zh, 4 - k, NZ)]
        return copy(piece, piece, gz_s.at[k - 1], gz_r.at[k - 1], at(zh_=rotate(zh, k, NZ)))

    def gy_copy(k):
        return copy(gz.at[4, k], gy.at[y], gy_s.at[k - 1], gy_r.at[k - 1], at(y_=rotate(y, k, NY)))

    def gy_arrival(k):
        piece = gy.at[rotate(y, 4 - k, NY)]
        return copy(piece, piece, gy_s.at[k - 1], gy_r.at[k - 1], at(y_=rotate(y, k, NY)))

    def gx_copy(x_):
        place = 2 * zl + core
        return copy(gy.at[4], gx.at[place], gx_s.at[x_], gx_r.at[place], (y, zh * 4 + x_, x))

    gz[zh, 0] = folded(weighed(y_own[0], 0, 0) + weighed(y_own[1], 1, 0))
    for k in (1, 3):
        gz[zh, k] = folded(weighed(y_send[0, k - 1], 0, k) + weighed(y_send[1, k - 1], 1, k))
    gz[zh, 2] = folded(weighed(y_send[0, 1], zl, 2))
    for k in (1, 2, 3):
        gz_copy(k).start()
    deliver(0)
    inv = inv_ref[...]
    rsum_ref[...] = spread(reduce_end(8)[:1]) * inv * inv / width
    for k in (1, 2, 3):
        gz_arrival(k).wait_recv()
    gz[4] = (gz[0] + gz[1]) + (gz[2] + gz[3])
    gy[y] = gz[4, 0]
    for k in (1, 2, 3):
        gy_copy(k).start()

    deliver(1)

    def owned(b):
        part = pl.ds(b * src, src)
        for k in (0, 1):
            copy(fin_send.at[0, part], fin.at[k, part], d3_s.at[b, 0], d3_r.at[b, k], at(core_=other)).wait_recv()
        dnormed = fin[0, part, :].astype(F32) + fin[1, part, :].astype(F32)
        own_gain = ext[rows : rows + 16, :].astype(F32)[:1]
        gs_ref[part, :] = own_gain * (wide(inv_ref[part, :]) * dnormed) - ext[part, :].astype(F32) * wide(
            rsum_ref[part, :]
        )

    for k in (1, 2, 3):
        gy_arrival(k).wait_recv()
    gy[4] = (gy[0] + gy[1]) + (gy[2] + gy[3])
    for x_ in range(NX):
        itself = jnp.logical_and(home, x == x_)

        @pl.when(itself)
        def _():
            place = 2 * zl + core
            pltpu.make_async_copy(gy.at[4], gx.at[place], gx_r.at[place]).start()

        @pl.when(jnp.logical_not(itself))
        def _():
            gx_copy(x_).start()

    owned(0)
    owned(1)

    def sent_w(c, carry):
        for up in (True, False):
            for stage in range(5):
                w_copy(stage, c, up).wait_send()
        for j in range(3):
            for b in range(batches):
                rs_copy(c, j, b).wait_send()
                ag_copy(c, j, b).wait_send()
        return carry

    lax.fori_loop(0, CHUNKS, sent_w, 0)

    @pl.when(jnp.logical_not(home))
    def _():
        s1_near.wait_send()

    for half in (0, 1):
        for up in (True, False):
            s2_direct(half, up).wait_send()
            s2_forward(half, up).wait_send()
        for k in range(4):
            s3_copy(half, k).wait_send()
        for b in range(batches):
            for k in range(4):
                d1_copy(b, half, k).wait_send()
            for k in (1, 3) if half else (1, 2, 3):
                d2_copy(b, half, k).wait_send()
            if half == 0:
                dz_copy(b).wait_send()

            @pl.when(jnp.logical_not(stays(half)))
            def _():
                d3_copy(b, half).wait_send()

    for k in (1, 2, 3):
        xt_copy(k).wait_send()
        gz_copy(k).wait_send()
        gy_copy(k).wait_send()
    for x_ in range(NX):

        @pl.when(jnp.logical_not(jnp.logical_and(home, x == x_)))
        def _():
            gx_copy(x_).wait_send()

    for k in range(4):
        copy(gy.at[4], gx.at[k], gx_s.at[0], gx_r.at[k], at(core_=other)).wait_recv()
    total = (gx[0] + gx[1]) + (gx[2] + gx[3])
    gg_ref[...] = jnp.concatenate([total[i : i + 1] for i in range(feats // 128)], axis=1)


def per_device(states, gain, kv_weight, queries, out_grad, src_len):
    batches, src, feats = states.shape
    tgt, heads_cols = queries.shape[2:]
    rows = batches * src
    cols = 2 * heads_cols // CHUNKS
    w = kv_weight.reshape(feats, 2 * heads_cols)
    ext = jnp.concatenate([states.reshape(rows, feats), jnp.broadcast_to(gain[None, :], (16, feats))], axis=0)
    vmem = pl.BlockSpec(memory_space=pltpu.VMEM)
    dma = pltpu.SemaphoreType.DMA
    out = pl.pallas_call(
        kernel,
        out_shape=(
            jax.ShapeDtypeStruct((batches, tgt, heads_cols), BF16),
            jax.ShapeDtypeStruct((batches, tgt, heads_cols), BF16),
            jax.ShapeDtypeStruct((rows, feats), F32),
            jax.ShapeDtypeStruct((1, feats), F32),
        ),
        in_specs=[pl.BlockSpec(memory_space=pl.ANY)] * 4 + [pl.BlockSpec(memory_space=pltpu.SMEM)],
        out_specs=[vmem] * 4,
        scratch_shapes=[
            pltpu.VMEM((rows + 16, feats), BF16),
            pltpu.VMEM((batches, tgt, heads_cols), BF16),
            pltpu.VMEM((batches, tgt, heads_cols), BF16),
            pltpu.VMEM((4, CHUNKS, feats, cols), BF16),
            pltpu.VMEM((2, CHUNKS, feats, cols), BF16),
            pltpu.VMEM((2, CHUNKS, feats // 2, cols), BF16),
            pltpu.VMEM((4, cols, feats), BF16),
            pltpu.VMEM((2, 4, rows + 16, feats), BF16),
            pltpu.VMEM((4, 4, rows, feats), BF16),
            pltpu.VMEM((CHUNKS, rows, cols), F32),
            pltpu.VMEM((CHUNKS, 3, rows, cols), BF16),
            pltpu.VMEM((CHUNKS, 3, rows, cols), BF16),
            pltpu.VMEM((CHUNKS, 4, rows, cols), BF16),
            pltpu.VMEM((4, 4, rows, feats), F32),
            pltpu.VMEM((2, 4, rows, feats), BF16),
            pltpu.VMEM((2, 4, rows, feats), BF16),
            pltpu.VMEM((rows, feats), BF16),
            pltpu.VMEM((rows, feats), BF16),
            pltpu.VMEM((2, 3, rows, feats), BF16),
            pltpu.VMEM((2, 3, rows, feats), BF16),
            pltpu.VMEM((2, rows, feats), F32),
            pltpu.VMEM((2, rows, feats), BF16),
            pltpu.VMEM((2, rows, feats), BF16),
            pltpu.VMEM((rows, 128), F32),
            pltpu.VMEM((16, 8, rows), F32),
            pltpu.VMEM((4, 8, rows), F32),
            pltpu.VMEM((5, 4, 8, 128), F32),
            pltpu.VMEM((5, 8, 128), F32),
            pltpu.VMEM((4, 8, 128), F32),
            pltpu.VMEM((rows, 128), F32),
            pltpu.VMEM((2, rows, 128), F32),
            pltpu.VMEM((rows, 128), F32),
            dma((4,)),
            dma((5, 2, CHUNKS)), dma((5, 2, CHUNKS)),
            dma((2,)), dma((2,)),
            dma((2, 2)), dma((2, 2)), dma((2, 2)), dma((2, 2)),
            dma((2, 4)), dma((2, 4)),
            dma((CHUNKS, 3, 2)), dma((CHUNKS, 3, 2)),
            dma((CHUNKS, 3, 2)), dma((CHUNKS, 3, 2)),
            dma((2, 2, 4)), dma((2, 2, 4)),
            dma((2,)), dma((2,)),
            dma((2, 2, 3)), dma((2, 2, 3)),
            dma((2, 2)), dma((2, 2)),
            dma((16,)), dma((16,)),
            dma((3,)), dma((3,)),
            dma((3,)), dma((3,)),
            dma((3,)), dma((3,)),
            dma((4,)), dma((4,)),
        ],
        compiler_params=pltpu.CompilerParams(
            collective_id=1, has_side_effects=True, vmem_limit_bytes=52 * 2**20
        ),
        name="cross_attention",
    )(
        w, ext, queries[0], out_grad[0], src_len
    )
    attended, grad_q, grad_states, grad_gain = out
    return attended[None], grad_q[None], grad_states.reshape(batches, src, feats), grad_gain[0]


def solution(mesh):
    return jax.shard_map(
        per_device,
        mesh=mesh,
        in_specs=(
            P("dp", None, ("section", "tensor")),
            P(("section", "tensor")),
            P("section", "dp", None, "tensor"),
            P("section", "dp", None, "tensor"),
            P("section", "dp", None, "tensor"),
            P("dp"),
        ),
        out_specs=(
            P("section", "dp", None, "tensor"),
            P("section", "dp", None, "tensor"),
            P("dp", None, ("section", "tensor")),
            P(("section", "tensor")),
        ),
        check_vma=False,
    )
```

```python
import jax
import jax.numpy as jnp
from jax import lax
from jax.experimental import pallas as pl
from jax.experimental.pallas import tpu as pltpu
from jax.sharding import PartitionSpec as P

MESH = pl.DeviceIdType.MESH
HEAD_DIM = 64
SCALE = HEAD_DIM ** (-0.5)
EPS = 1e-06
NX, NY, NZ = 4, 4, 4
CHUNKS = 4
F32, BF16 = jnp.float32, jnp.bfloat16


def rotate(a, by, n):
    return lax.rem(a + by, n)


def kernel(
    w_ref, states_in, gain_in, q_in, og_in, len_in,
    att_ref, gq_ref, gs_ref, gg_ref,
    len_ref, ext, q_ref, og_ref, wg, through, through_half, turned, raw, a, own_part, part_send, rs_recv, ag, dn, core_send, core_recv, z_send, z_recv, y_send, y_recv,
    y_own, fin_send, fin, racc, small, xtot, gz, gy, gx, inv_ref, piece_inv, rsum_ref,
    local_sem, w_s, w_r, s1_s, s1_r, s2_s, s2_r, s2f_s, s2f_r, s3_s, s3_r, rs_s, rs_r, ag_s, ag_r,
    d1_s, d1_r, dz_s, dz_r, d2_s, d2_r, d3_s, d3_r, sm_s, sm_r, xt_s, xt_r, gz_s, gz_r, gy_s, gy_r, gx_s, gx_r,
):
    y, d, t = lax.axis_index("section"), lax.axis_index("dp"), lax.axis_index("tensor")
    zh, x, zl, core = d // 4, lax.rem(d, 4), t // 2, lax.rem(t, 2)
    rows, feats = gs_ref.shape
    batches = q_ref.shape[0]
    src = rows // batches
    cols = wg.shape[3]
    heads_cols = q_ref.shape[2]
    width = NX * NZ * feats

    def at(y_=None, zh_=None, x_=None, zl_=None, core_=None):
        pick = lambda new, old: old if new is None else new
        return (pick(y_, y), pick(zh_, zh) * 4 + pick(x_, x), pick(zl_, zl) * 2 + pick(core_, core))

    def copy(src_ref, dst_ref, send, recv, to):
        return pltpu.make_async_remote_copy(
            src_ref=src_ref, dst_ref=dst_ref, send_sem=send, recv_sem=recv, device_id=to, device_id_type=MESH
        )

    other = 1 - core
    home = t == x

    load_ext = pltpu.make_async_copy(states_in, ext.at[:rows], local_sem.at[0])
    load_gain = pltpu.make_async_copy(gain_in, ext.at[rows : rows + 16], local_sem.at[4])
    load_len = pltpu.make_async_copy(len_in, len_ref, local_sem.at[5])
    load_q = pltpu.make_async_copy(q_in, q_ref, local_sem.at[1])
    load_og = pltpu.make_async_copy(og_in, og_ref, local_sem.at[2])
    load_ext.start()
    load_gain.start()
    load_len.start()
    load_q.start()
    load_og.start()
    barrier = pltpu.get_barrier_semaphore()

    def greet(to):
        pl.semaphore_signal(barrier, inc=1, device_id=to, device_id_type=MESH)

    for k in (1, 2, 3):
        greet(at(zh_=rotate(zh, k, NZ)))
        greet(at(y_=rotate(y, k, NY)))
        greet(at(x_=rotate(x, k, NX)))
    greet(at(core_=other))
    above = at(zh_=rotate(zh, zl, NZ), zl_=1 - zl)
    below = at(zh_=rotate(zh, 3 + zl, NZ), zl_=1 - zl)
    greet(above)
    greet(below)
    for zl_ in (0, 1):
        for core_ in (0, 1):
            itself = jnp.logical_and(home, jnp.logical_and(zl == zl_, core == core_))

            @pl.when(jnp.logical_not(itself))
            def _():
                greet(at(x_=t, zl_=zl_, core_=core_))

    for x_ in range(NX):

        @pl.when(jnp.logical_not(jnp.logical_and(home, x == x_)))
        def _():
            greet((y, zh * 4 + x_, x))

    @pl.when(jnp.logical_not(home))
    def _():
        pl.semaphore_wait(barrier, 20)

    @pl.when(home)
    def _():
        pl.semaphore_wait(barrier, 18)

    x_core = lax.rem(x, 2)

    def w_lanes(c):
        k = pl.ds(pl.multiple_of(c * 128, 128), 128)
        v = pl.ds(pl.multiple_of(heads_cols + c * 128, 128), 128)
        return ((k, pl.ds(0, 128)), (v, pl.ds(128, 128)))

    def w_copy(stage, c, up):
        half = feats // 2
        part, rest = pl.ds(0 if up else half, half), pl.ds(half if up else 0, half)
        way, direct = int(up), wg.at[3 if up else 1, c]
        here, there = (
            (through.at[way, c], through.at[way, c]),
            (through.at[way, c, part], direct.at[part]),
            (direct.at[part], through_half.at[way, c]),
            (through_half.at[way, c], wg.at[2, c, part]),
            (through.at[way, c, rest], direct.at[rest]),
        )[stage]
        return copy(here, there, w_s.at[stage], w_r.at[stage, way, c], above if up else below)

    def w_send(c):
        for up in (True, False):
            for here, there in w_lanes(c):
                copy(
                    w_ref.at[:, here], through.at[int(up), c, :, there],
                    w_s.at[0], w_r.at[0, int(up), c], above if up else below,
                ).start()

    def hop(stage, c):
        for up in (True, False):
            w_copy(stage, c, up).wait_recv()
            w_copy(stage + 1, c, up).start()
            if stage == 0:
                w_copy(4, c, up).start()

    load_ext.wait()
    load_gain.wait()

    def s1_copy(z, to):
        return copy(ext, raw.at[x // 2, y], s1_s.at[z], s1_r.at[x // 2], to)

    s1_far = s1_copy(1, at(x_=t, zl_=1 - zl, core_=x_core))
    s1_near = s1_copy(0, at(x_=t, core_=x_core))
    s1_local = pltpu.make_async_copy(ext, raw.at[x // 2, y], s1_r.at[x // 2])
    s1_far.start()

    @pl.when(jnp.logical_not(home))
    def _():
        s1_near.start()

    @pl.when(home)
    def _():
        s1_local.start()

    for c in range(CHUNKS):
        for here, there in w_lanes(c):
            pltpu.make_async_copy(w_ref.at[:, here], wg.at[0, c, :, there], local_sem.at[3]).start()

    h = ext[:rows, :].astype(F32)
    squares = h * h

    def total_lanes(v):
        acc = v[:, :128]
        for k in range(128, v.shape[1], 128):
            acc = acc + v[:, k : k + 128]
        return jnp.broadcast_to(jnp.sum(acc.T, axis=0, keepdims=True), (8, rows))

    def spread(row):
        return jnp.broadcast_to(row, (128, rows)).T

    def reduce_start(base, v):
        small[base] = v
        c = copy(small.at[base], small.at[base + 1], sm_s.at[base], sm_r.at[base + 1], at(core_=other))
        c.start()

    def reduce_zl(base):
        copy(small.at[base], small.at[base + 1], sm_s.at[base], sm_r.at[base + 1], at(core_=other)).wait()
        small[base + 2] = small[base] + small[base + 1]
        copy(small.at[base + 2], small.at[base + 3], sm_s.at[base + 2], sm_r.at[base + 3], at(zl_=1 - zl)).start()

    def reduce_y_copies(base):
        return [
            copy(
                small.at[base + 4], small.at[base + 4 + k], sm_s.at[base + 4 + k], sm_r.at[base + 4 + k],
                at(y_=rotate(y, k, NY)),
            )
            for k in (1, 2, 3)
        ]

    def reduce_y(base):
        copy(small.at[base + 2], small.at[base + 3], sm_s.at[base + 2], sm_r.at[base + 3], at(zl_=1 - zl)).wait()
        small[base + 4] = small[base + 2] + small[base + 3]
        for c in reduce_y_copies(base):
            c.start()

    def reduce_end(base):
        for c in reduce_y_copies(base):
            c.wait()
        return (small[base + 4] + small[base + 5]) + (small[base + 6] + small[base + 7])

    reduce_start(0, total_lanes(squares))

    cut = 9 * 16
    parts = (pl.ds(0, cut), pl.ds(cut, raw.shape[2] - cut))

    def s2_direct(half, up):
        to = at(y_=rotate(y, 1 if up else 3, NY))
        piece = raw.at[half, y]
        return copy(piece, piece, s2_s.at[0], s2_r.at[half, int(up)], to)

    def s2_arrival(half, up):
        to = at(y_=rotate(y, 1 if up else 3, NY))
        piece = raw.at[half, rotate(y, 3 if up else 1, NY)]
        return copy(piece, piece, s2_s.at[0], s2_r.at[half, int(up)], to)

    def s2_forward(half, up):
        to = at(y_=rotate(y, 1 if up else 3, NY))
        piece = raw.at[half, rotate(y, 3 if up else 1, NY), parts[0 if up else 1]]
        return copy(piece, piece, s2f_s.at[0], s2f_r.at[half, int(up)], to)

    def s2_last(half, up):
        to = at(y_=rotate(y, 1 if up else 3, NY))
        piece = raw.at[half, rotate(y, 2, NY), parts[0 if up else 1]]
        return copy(piece, piece, s2f_s.at[0], s2f_r.at[half, int(up)], to)

    def s3_copy(half, k):
        piece = a.at[core + 2 * half, rotate(y, 4 - k, NY)]
        return copy(piece, piece, s3_s.at[0], s3_r.at[0], at(core_=other))

    def s3_all():
        pieces = a.at[pl.ds(0, 2)]
        return copy(pieces, pieces, s3_s.at[0], s3_r.at[0], at(core_=other))

    def normalise(half, k):
        s = rotate(y, 4 - k, NY)
        g = raw[half, s, rows : rows + 16, :].astype(F32)[:1]
        v = raw[half, s, :rows, :].astype(F32) * wide(piece_inv[half]) * g
        a[core + 2 * half, s] = v.astype(BF16)
        s3_copy(half, k).start()

    def wide(v):
        return jnp.concatenate([v] * (feats // 128), axis=1)

    def inverse(row):
        return 1.0 / jnp.sqrt(spread(row) / width + EPS)

    def xt_copy(k):
        return copy(xtot.at[x], xtot.at[x], xt_s.at[k - 1], xt_r.at[k - 1], at(x_=rotate(x, k, NX)))

    def xt_arrival(k):
        piece = xtot.at[rotate(x, 4 - k, NX)]
        return copy(piece, piece, xt_s.at[k - 1], xt_r.at[k - 1], at(x_=rotate(x, k, NX)))

    reduce_zl(0)
    s1_far.wait_send()
    w_send(0)
    reduce_y(0)
    for half in (0, 1):
        copy(ext, raw.at[half, y], s1_s.at[0], s1_r.at[half], at(core_=other)).wait_recv()
        for up in (True, False):
            s2_direct(half, up).start()
    w_send(1)
    xtot[x] = reduce_end(0)
    for k in (1, 2, 3):
        xt_copy(k).start()
    hop(0, 0)
    for k in (1, 2, 3):
        xt_arrival(k).wait_recv()
    inv_ref[...] = inverse(xtot[x][:1])
    for half in (0, 1):
        piece_inv[half] = inverse(xtot[core + 2 * half][:1])
    racc[...] = jnp.zeros_like(racc)
    for half in (0, 1):
        normalise(half, 0)
    hop(0, 1)
    for half in (0, 1):
        for up in (True, False):
            s2_arrival(half, up).wait_recv()
            s2_forward(half, up).start()
    hop(1, 0)
    w_send(2)
    for half in (0, 1):
        for k in (1, 3):
            normalise(half, k)
    hop(1, 1)
    for half in (0, 1):
        for up in (True, False):
            s2_last(half, up).wait_recv()
        normalise(half, 2)
    hop(2, 0)
    load_len.wait()
    load_q.wait()
    load_og.wait()
    pltpu.make_async_copy(wg.at[0], wg.at[0], local_sem.at[3]).wait()
    s3_all().wait_recv()
    hop(0, 2)
    hop(2, 1)

    def sequence(b):
        return pl.ds(pl.multiple_of(b * src, src), src)

    def rs_copy(c, j, b):
        part = sequence(b)
        return copy(
            part_send.at[c, j, part], rs_recv.at[c, j, part], rs_s.at[0], rs_r.at[c, b],
            at(x_=rotate(x, 1 + j, NX)),
        )

    def rs_arrived(c, b):
        pieces = rs_recv.at[c, :, sequence(b)]
        copy(pieces, pieces, rs_s.at[0], rs_r.at[c, b], at(core_=other)).wait_recv()

    def ag_copy(c, j, b):
        piece = ag.at[c, x, sequence(b)]
        return copy(piece, piece, ag_s.at[0], ag_r.at[c, b], at(x_=rotate(x, 1 + j, NX)))

    def ag_arrived(c, b):
        pieces = ag.at[c, pl.ds(0, 3), sequence(b)]
        copy(pieces, pieces, ag_s.at[0], ag_r.at[c, b], at(core_=other)).wait_recv()

    def project(c):
        for up in (True, False):
            w_copy(4, c, up).wait_recv()
            w_copy(3, c, up).wait_recv()

        def one(j, b):
            xs = rotate(x, 1 + j, NX)
            acc = jnp.zeros((src, cols), F32)
            for r in range(4):
                acc = acc + jnp.dot(a[xs, rotate(zh, r, NZ), sequence(b), :], wg[r, c], preferred_element_type=F32)
            return acc

        def sequences(b, carry):
            for j in range(3):
                part_send[c, j, sequence(b), :] = one(j, b).astype(BF16)
                rs_copy(c, j, b).start()
            own_part[c, sequence(b), :] = one(3, b)
            return carry

        lax.fori_loop(0, batches, sequences, 0)

    lane = lax.broadcasted_iota(jnp.int32, (1, 128), 1)
    first = lane < HEAD_DIM
    place = lax.rem(lax.broadcasted_iota(jnp.int32, (1, 2 * src), 1), src)

    def two_heads(v):
        return jnp.concatenate([jnp.where(first, v, 0.0), jnp.where(first, 0.0, v)], axis=0).astype(BF16)

    def per_head(v, f):
        return jnp.concatenate([f(v[:, :src]), f(v[:, src:])], axis=1)

    def dot_t(m, n):
        return lax.dot_general(m, n, (((1,), (1,)), ((), ())), preferred_element_type=F32)

    def t_dot(m, n):
        return lax.dot_general(m, n, (((0,), (0,)), ((), ())), preferred_element_type=F32)

    def attend(c):
        lanes = pl.ds(pl.multiple_of(c * 128, 128), 128)

        def one(b, carry):
            at_rows = sequence(b)
            kv_b = own_part[c, at_rows, :]
            rs_arrived(c, b)
            for j in range(3):
                kv_b = kv_b + rs_recv[c, j, at_rows, :].astype(F32)
            keys = two_heads(kv_b[:, :128].astype(BF16).astype(F32))
            values = two_heads(kv_b[:, 128:].astype(BF16).astype(F32))
            query, cotan = q_ref[b, :, lanes], og_ref[b, :, lanes]
            expo = jnp.where(place < len_ref[b], jnp.exp(dot_t(query, keys) * SCALE), 0.0)
            probs = per_head(expo, lambda e: e / jnp.sum(e, axis=-1, keepdims=True))
            probs_b = probs.astype(BF16)
            att_ref[b, :, lanes] = jnp.dot(probs_b, values, preferred_element_type=F32).astype(BF16)
            dprob = dot_t(cotan, values)
            delta = per_head(
                probs * dprob, lambda e: jnp.broadcast_to(jnp.sum(e, axis=-1, keepdims=True), e.shape)
            )
            dscore = (probs * (dprob - delta) * SCALE).astype(BF16)
            gq_ref[b, :, lanes] = jnp.dot(dscore, keys, preferred_element_type=F32).astype(BF16)
            dkey, dvalue = t_dot(dscore, query), t_dot(probs_b, cotan)
            dkv = jnp.concatenate(
                [jnp.where(first, dkey[:src], dkey[src:]), jnp.where(first, dvalue[:src], dvalue[src:])], axis=1
            ).astype(BF16)
            ag[c, x, at_rows, :] = dkv
            for j in range(3):
                ag_copy(c, j, b).start()
            product = dkv.astype(F32) * kv_b
            racc[at_rows, :] = racc[at_rows, :] + (product[:, :128] + product[:, 128:])
            return carry

        lax.fori_loop(0, batches, one, 0)

    def back(chunks):
        for c in chunks:
            for b in range(batches):
                ag_arrived(c, b)

        def one(r, carry):
            term = dot_t(ag[chunks[0]].reshape(4 * rows, cols), wg[r, chunks[0]])
            for c in chunks[1:]:
                term = term + dot_t(ag[c].reshape(4 * rows, cols), wg[r, c])
            for xs in range(4):
                mine = term[xs * rows : (xs + 1) * rows]
                dn[xs, r] = mine if chunks[0] == 0 else dn[xs, r] + mine
            return carry

        lax.fori_loop(0, 4, one, 0)

    project(0)
    hop(1, 2)
    w_send(3)
    project(1)
    attend(0)
    hop(2, 2)
    attend(1)
    hop(0, 3)
    back((0,))
    project(2)
    hop(1, 3)
    back((1,))
    hop(2, 3)
    attend(2)
    project(3)
    attend(3)
    reduce_start(8, total_lanes(racc[...]))
    last = CHUNKS - 1
    for r in range(4):
        turned[r] = wg[r, last].T
    back((2,))

    def d1_copy(b, half, k):
        part = sequence(b)
        return copy(
            core_send.at[half, k, part], core_recv.at[half, k, part],
            d1_s.at[0], d1_r.at[b, half, k], at(core_=other),
        )

    SLOT = {1: 0, 3: 1, 2: 2}

    def d2_copy(b, half, k):
        part, slot, two = sequence(b), SLOT[k], int(k == 2)
        return copy(
            y_send.at[half, slot, part], y_recv.at[half, slot, part], d2_s.at[two], d2_r.at[two, b],
            at(y_=rotate(y, k, NY)),
        )

    def d2_arrived(b):
        pieces = y_recv.at[:, pl.ds(0, 2), sequence(b)]
        copy(pieces, pieces, d2_s.at[0], d2_r.at[0, b], at(core_=other)).wait_recv()
        d2_copy(b, 0, 2).wait_recv()

    def whole(b, xs, k):
        part = sequence(b)
        r = lax.rem(y + k + NZ - zh, NZ)
        return dn[xs, r, part, :] + jnp.dot(ag[last, xs, part, :], turned[r], preferred_element_type=F32)

    def dz_copy(b):
        part = sequence(b)
        return copy(z_send.at[part], z_recv.at[part], dz_s.at[b], dz_r.at[b], at(zl_=1 - zl))

    def chip_sum(b, half, k):
        v = whole(b, core + 2 * half, k)
        d1_copy(b, half, k).wait_recv()
        return v + core_recv[half, k, sequence(b), :].astype(F32)

    def cores(b):
        ag_arrived(last, b)
        part = sequence(b)
        for k in (2, 1, 3, 0):
            for half in (0, 1):
                core_send[half, k, part, :] = whole(b, other + 2 * half, k).astype(BF16)
                d1_copy(b, half, k).start()
        z_send[part, :] = chip_sum(b, 1 - zl, 2).astype(BF16)
        dz_copy(b).start()

    def one_step(b):
        for half in (0, 1):
            for k in (1, 3):
                y_send[half, SLOT[k], sequence(b), :] = chip_sum(b, half, k).astype(BF16)
                d2_copy(b, half, k).start()

    def two_steps(b):
        part = sequence(b)
        v = chip_sum(b, zl, 2)
        dz_copy(b).wait_recv()
        y_send[0, 2, part, :] = (v + z_recv[part, :].astype(F32)).astype(BF16)
        d2_copy(b, 0, 2).start()

    cores(0)
    one_step(0)
    reduce_zl(8)
    cores(1)
    two_steps(0)
    reduce_y(8)
    one_step(1)
    two_steps(1)
    for b in range(batches):
        for half in (0, 1):
            y_own[half, sequence(b), :] = chip_sum(b, half, 0)

    def d3_copy(b, half):
        part = pl.ds(b * src, src)
        to = (y, zh * 4 + core + 2 * half, x)
        return copy(fin_send.at[half, part], fin.at[zl, part], d3_s.at[b, half], d3_r.at[b, zl], to)

    def stays(half):
        return jnp.logical_and(home, x // 2 == half)

    def deliver(b):
        part = pl.ds(b * src, src)
        d2_arrived(b)
        for half in (0, 1):
            v = y_own[half, part, :]
            for k in (1, 3):
                v = v + y_recv[half, SLOT[k], part, :].astype(F32)
            v = v + jnp.where(zl == half, y_recv[0, 2, part, :].astype(F32), 0.0)
            fin_send[half, part, :] = v.astype(BF16)

            @pl.when(stays(half))
            def _():
                pltpu.make_async_copy(fin_send.at[half, part], fin.at[zl, part], d3_r.at[b, zl]).start()

            @pl.when(jnp.logical_not(stays(half)))
            def _():
                d3_copy(b, half).start()

    def weighed(v, half, k):
        hidden = raw[half, rotate(y, k, NY), :rows, :].astype(F32) * wide(piece_inv[half])
        return jnp.sum(v.astype(F32) * hidden, axis=0, keepdims=True)

    def folded(v):
        lanes = [v[:, i : i + 128] for i in range(0, feats, 128)]
        return jnp.concatenate(lanes + lanes, axis=0)

    def gz_copy(k):
        return copy(gz.at[zh], gz.at[zh], gz_s.at[k - 1], gz_r.at[k - 1], at(zh_=rotate(zh, k, NZ)))

    def gz_arrival(k):
        piece = gz.at[rotate(zh, 4 - k, NZ)]
        return copy(piece, piece, gz_s.at[k - 1], gz_r.at[k - 1], at(zh_=rotate(zh, k, NZ)))

    def gy_copy(k):
        return copy(gz.at[4, k], gy.at[y], gy_s.at[k - 1], gy_r.at[k - 1], at(y_=rotate(y, k, NY)))

    def gy_arrival(k):
        piece = gy.at[rotate(y, 4 - k, NY)]
        return copy(piece, piece, gy_s.at[k - 1], gy_r.at[k - 1], at(y_=rotate(y, k, NY)))

    def gx_copy(x_):
        place = 2 * zl + core
        return copy(gy.at[4], gx.at[place], gx_s.at[x_], gx_r.at[place], (y, zh * 4 + x_, x))

    gz[zh, 0] = folded(weighed(y_own[0], 0, 0) + weighed(y_own[1], 1, 0))
    for k in (1, 3):
        gz[zh, k] = folded(weighed(y_send[0, SLOT[k]], 0, k) + weighed(y_send[1, SLOT[k]], 1, k))
    gz[zh, 2] = folded(weighed(y_send[0, 2], zl, 2))
    for k in (1, 2, 3):
        gz_copy(k).start()
    deliver(0)
    inv = inv_ref[...]
    rsum_ref[...] = spread(reduce_end(8)[:1]) * inv * inv / width
    for k in (1, 2, 3):
        gz_arrival(k).wait_recv()
    gz[4] = (gz[0] + gz[1]) + (gz[2] + gz[3])
    gy[y] = gz[4, 0]
    for k in (1, 2, 3):
        gy_copy(k).start()

    def all_sent(pieces, sem, arrived):
        copy(pieces, pieces, sem, arrived, at(core_=other)).wait_send()

    all_sent(through, w_s.at[0], w_r.at[0, 0, 0])
    for stage in range(1, 5):
        all_sent(through_half, w_s.at[stage], w_r.at[stage, 0, 0])
    all_sent(part_send, rs_s.at[0], rs_r.at[0, 0])
    all_sent(ag.at[:, pl.ds(0, 3)], ag_s.at[0], ag_r.at[0, 0])
    all_sent(raw.at[0], s2_s.at[0], s2_r.at[0, 0])
    all_sent(raw.at[0, pl.ds(0, 2)], s2f_s.at[0], s2f_r.at[0, 0])
    s3_all().wait_send()
    all_sent(core_send, d1_s.at[0], d1_r.at[0, 0, 0])

    @pl.when(jnp.logical_not(home))
    def _():
        s1_near.wait_send()

    for k in (1, 2, 3):
        xt_copy(k).wait_send()
    deliver(1)

    def owned(b):
        part = pl.ds(b * src, src)
        for k in (0, 1):
            copy(fin_send.at[0, part], fin.at[k, part], d3_s.at[b, 0], d3_r.at[b, k], at(core_=other)).wait_recv()
        dnormed = fin[0, part, :].astype(F32) + fin[1, part, :].astype(F32)
        own_gain = ext[rows : rows + 16, :].astype(F32)[:1]
        gs_ref[part, :] = own_gain * (wide(inv_ref[part, :]) * dnormed) - ext[part, :].astype(F32) * wide(
            rsum_ref[part, :]
        )

    for k in (1, 2, 3):
        gy_arrival(k).wait_recv()
    gy[4] = (gy[0] + gy[1]) + (gy[2] + gy[3])
    for x_ in range(NX):
        itself = jnp.logical_and(home, x == x_)

        @pl.when(itself)
        def _():
            place = 2 * zl + core
            pltpu.make_async_copy(gy.at[4], gx.at[place], gx_r.at[place]).start()

        @pl.when(jnp.logical_not(itself))
        def _():
            gx_copy(x_).start()

    owned(0)
    owned(1)

    all_sent(y_send.at[:, pl.ds(0, 2)], d2_s.at[0], d2_r.at[0, 0])
    all_sent(y_send.at[0, 2], d2_s.at[1], d2_r.at[1, 0])
    for b in range(batches):
        dz_copy(b).wait_send()
        for half in (0, 1):

            @pl.when(jnp.logical_not(stays(half)))
            def _():
                d3_copy(b, half).wait_send()

    for k in (1, 2, 3):
        gz_copy(k).wait_send()
        gy_copy(k).wait_send()
    for x_ in range(NX):

        @pl.when(jnp.logical_not(jnp.logical_and(home, x == x_)))
        def _():
            gx_copy(x_).wait_send()

    for k in range(4):
        copy(gy.at[4], gx.at[k], gx_s.at[0], gx_r.at[k], at(core_=other)).wait_recv()
    total = (gx[0] + gx[1]) + (gx[2] + gx[3])
    gg_ref[...] = jnp.concatenate([total[i : i + 1] for i in range(feats // 128)], axis=1)


def per_device(states, gain, kv_weight, queries, out_grad, src_len):
    batches, src, feats = states.shape
    tgt, heads_cols = queries.shape[2:]
    rows = batches * src
    cols = 2 * heads_cols // CHUNKS
    w = kv_weight.reshape(feats, 2 * heads_cols)
    gains = jnp.broadcast_to(gain[None, :], (16, feats))
    vmem = pl.BlockSpec(memory_space=pltpu.VMEM)
    dma = pltpu.SemaphoreType.DMA
    out = pl.pallas_call(
        kernel,
        out_shape=(
            jax.ShapeDtypeStruct((batches, tgt, heads_cols), BF16),
            jax.ShapeDtypeStruct((batches, tgt, heads_cols), BF16),
            jax.ShapeDtypeStruct((rows, feats), F32),
            jax.ShapeDtypeStruct((1, feats), F32),
        ),
        in_specs=[pl.BlockSpec(memory_space=pl.ANY)] * 6,
        out_specs=[vmem] * 4,
        scratch_shapes=[
            pltpu.SMEM((batches,), jnp.int32),
            pltpu.VMEM((rows + 16, feats), BF16),
            pltpu.VMEM((batches, tgt, heads_cols), BF16),
            pltpu.VMEM((batches, tgt, heads_cols), BF16),
            pltpu.VMEM((4, CHUNKS, feats, cols), BF16),
            pltpu.VMEM((2, CHUNKS, feats, cols), BF16),
            pltpu.VMEM((2, CHUNKS, feats // 2, cols), BF16),
            pltpu.VMEM((4, cols, feats), BF16),
            pltpu.VMEM((2, 4, rows + 16, feats), BF16),
            pltpu.VMEM((4, 4, rows, feats), BF16),
            pltpu.VMEM((CHUNKS, rows, cols), F32),
            pltpu.VMEM((CHUNKS, 3, rows, cols), BF16),
            pltpu.VMEM((CHUNKS, 3, rows, cols), BF16),
            pltpu.VMEM((CHUNKS, 4, rows, cols), BF16),
            pltpu.VMEM((4, 4, rows, feats), F32),
            pltpu.VMEM((2, 4, rows, feats), BF16),
            pltpu.VMEM((2, 4, rows, feats), BF16),
            pltpu.VMEM((rows, feats), BF16),
            pltpu.VMEM((rows, feats), BF16),
            pltpu.VMEM((2, 3, rows, feats), BF16),
            pltpu.VMEM((2, 3, rows, feats), BF16),
            pltpu.VMEM((2, rows, feats), F32),
            pltpu.VMEM((2, rows, feats), BF16),
            pltpu.VMEM((2, rows, feats), BF16),
            pltpu.VMEM((rows, 128), F32),
            pltpu.VMEM((16, 8, rows), F32),
            pltpu.VMEM((4, 8, rows), F32),
            pltpu.VMEM((5, 4, 8, 128), F32),
            pltpu.VMEM((5, 8, 128), F32),
            pltpu.VMEM((4, 8, 128), F32),
            pltpu.VMEM((rows, 128), F32),
            pltpu.VMEM((2, rows, 128), F32),
            pltpu.VMEM((rows, 128), F32),
            dma((6,)),
            dma((5,)), dma((5, 2, CHUNKS)),
            dma((2,)), dma((2,)),
            dma((1,)), dma((2, 2)), dma((1,)), dma((2, 2)),
            dma((1,)), dma((1,)),
            dma((1,)), dma((CHUNKS, 2)),
            dma((1,)), dma((CHUNKS, 2)),
            dma((1,)), dma((2, 2, 4)),
            dma((2,)), dma((2,)),
            dma((2,)), dma((2, 2)),
            dma((2, 2)), dma((2, 2)),
            dma((16,)), dma((16,)),
            dma((3,)), dma((3,)),
            dma((3,)), dma((3,)),
            dma((3,)), dma((3,)),
            dma((4,)), dma((4,)),
        ],
        compiler_params=pltpu.CompilerParams(
            collective_id=1, has_side_effects=True, vmem_limit_bytes=52 * 2**20
        ),
        name="cross_attention",
    )(
        w, states.reshape(rows, feats), gains, queries[0], out_grad[0], src_len
    )
    attended, grad_q, grad_states, grad_gain = out
    return attended[None], grad_q[None], grad_states.reshape(batches, src, feats), grad_gain[0]


def solution(mesh):
    return jax.shard_map(
        per_device,
        mesh=mesh,
        in_specs=(
            P("dp", None, ("section", "tensor")),
            P(("section", "tensor")),
            P("section", "dp", None, "tensor"),
            P("section", "dp", None, "tensor"),
            P("section", "dp", None, "tensor"),
            P("dp"),
        ),
        out_specs=(
            P("section", "dp", None, "tensor"),
            P("section", "dp", None, "tensor"),
            P("dp", None, ("section", "tensor")),
            P(("section", "tensor")),
        ),
        check_vma=False,
    )
```

```python
import jax
import jax.numpy as jnp
from jax import lax
from jax.experimental import pallas as pl
from jax.experimental.pallas import tpu as pltpu
from jax.sharding import PartitionSpec as P

MESH = pl.DeviceIdType.MESH
HEAD_DIM = 64
SCALE = HEAD_DIM ** (-0.5)
EPS = 1e-06
NX, NY, NZ = 4, 4, 4
CHUNKS = 4
F32, BF16 = jnp.float32, jnp.bfloat16


def rotate(a, by, n):
    return lax.rem(a + by, n)


def kernel(
    w_ref, states_in, gain_in, q_in, og_in, len_in,
    att_ref, gq_ref, gs_ref, gg_ref,
    len_ref, ext, q_ref, og_ref, wg, through, through_half, turned, raw, a, own_part, part_send, rs_recv, ag, dn, core_send, core_recv, z_send, z_recv, y_send, y_recv,
    y_own, fin_send, fin, racc, small, xtot, gz, gy, gx, inv_ref, piece_inv, rsum_ref,
    local_sem, w_s, w_r, s1_s, s1_r, s2_s, s2_r, s2f_s, s2f_r, s3_s, s3_r, rs_s, rs_r, ag_s, ag_r,
    d1_s, d1_r, dz_s, dz_r, d2_s, d2_r, d3_s, d3_r, sm_s, sm_r, xt_s, xt_r, gz_s, gz_r, gy_s, gy_r, gx_s, gx_r,
):
    y, d, t = lax.axis_index("section"), lax.axis_index("dp"), lax.axis_index("tensor")
    zh, x, zl, core = d // 4, lax.rem(d, 4), t // 2, lax.rem(t, 2)
    rows, feats = gs_ref.shape
    batches = q_ref.shape[0]
    src = rows // batches
    cols = wg.shape[3]
    heads_cols = q_ref.shape[2]
    width = NX * NZ * feats

    def at(y_=None, zh_=None, x_=None, zl_=None, core_=None):
        pick = lambda new, old: old if new is None else new
        return (pick(y_, y), pick(zh_, zh) * 4 + pick(x_, x), pick(zl_, zl) * 2 + pick(core_, core))

    def copy(src_ref, dst_ref, send, recv, to):
        return pltpu.make_async_remote_copy(
            src_ref=src_ref, dst_ref=dst_ref, send_sem=send, recv_sem=recv, device_id=to, device_id_type=MESH
        )

    other = 1 - core
    home = t == x

    load_ext = pltpu.make_async_copy(states_in, ext.at[:rows], local_sem.at[0])
    load_gain = pltpu.make_async_copy(gain_in, ext.at[rows : rows + 16], local_sem.at[4])
    load_len = pltpu.make_async_copy(len_in, len_ref, local_sem.at[5])
    load_q = pltpu.make_async_copy(q_in, q_ref, local_sem.at[1])
    load_og = pltpu.make_async_copy(og_in, og_ref, local_sem.at[2])
    load_ext.start()
    load_gain.start()
    load_len.start()
    load_q.start()
    load_og.start()
    barrier = pltpu.get_barrier_semaphore()

    def greet(to):
        pl.semaphore_signal(barrier, inc=1, device_id=to, device_id_type=MESH)

    for k in (1, 2, 3):
        greet(at(zh_=rotate(zh, k, NZ)))
        greet(at(y_=rotate(y, k, NY)))
        greet(at(x_=rotate(x, k, NX)))
    greet(at(core_=other))
    above = at(zh_=rotate(zh, zl, NZ), zl_=1 - zl)
    below = at(zh_=rotate(zh, 3 + zl, NZ), zl_=1 - zl)
    greet(above)
    greet(below)
    for zl_ in (0, 1):
        for core_ in (0, 1):
            itself = jnp.logical_and(home, jnp.logical_and(zl == zl_, core == core_))

            @pl.when(jnp.logical_not(itself))
            def _():
                greet(at(x_=t, zl_=zl_, core_=core_))

    for x_ in range(NX):

        @pl.when(jnp.logical_not(jnp.logical_and(home, x == x_)))
        def _():
            greet((y, zh * 4 + x_, x))

    @pl.when(jnp.logical_not(home))
    def _():
        pl.semaphore_wait(barrier, 20)

    @pl.when(home)
    def _():
        pl.semaphore_wait(barrier, 18)

    x_core = lax.rem(x, 2)

    def w_lanes(c):
        k = pl.ds(pl.multiple_of(c * 128, 128), 128)
        v = pl.ds(pl.multiple_of(heads_cols + c * 128, 128), 128)
        return ((k, pl.ds(0, 128)), (v, pl.ds(128, 128)))

    def w_copy(stage, c, up):
        half = feats // 2
        part, rest = pl.ds(0 if up else half, half), pl.ds(half if up else 0, half)
        way, direct = int(up), wg.at[3 if up else 1, c]
        here, there = (
            (through.at[way, c], through.at[way, c]),
            (through.at[way, c, part], direct.at[part]),
            (direct.at[part], through_half.at[way, c]),
            (through_half.at[way, c], wg.at[2, c, part]),
            (through.at[way, c, rest], direct.at[rest]),
        )[stage]
        return copy(here, there, w_s.at[stage], w_r.at[stage, way, c], above if up else below)

    def w_send_way(c, up):
        for here, there in w_lanes(c):
            copy(
                w_ref.at[:, here], through.at[int(up), c, :, there],
                w_s.at[0], w_r.at[0, int(up), c], above if up else below,
            ).start()

    def w_send(c):
        for up in (True, False):
            w_send_way(c, up)

    def w_send_first(outward):
        for up in (True, False):

            @pl.when((zl == int(up)) if outward else (zl != int(up)))
            def _():
                w_send_way(0, up)

    def hop(stage, c):
        for up in (True, False):
            w_copy(stage, c, up).wait_recv()
            w_copy(stage + 1, c, up).start()
            if stage == 0:
                w_copy(4, c, up).start()

    load_ext.wait()
    load_gain.wait()

    def s1_copy(z, to):
        return copy(ext, raw.at[x // 2, y], s1_s.at[z], s1_r.at[x // 2], to)

    s1_far = s1_copy(1, at(x_=t, zl_=1 - zl, core_=x_core))
    s1_near = s1_copy(0, at(x_=t, core_=x_core))
    s1_local = pltpu.make_async_copy(ext, raw.at[x // 2, y], s1_r.at[x // 2])
    s1_far.start()

    @pl.when(jnp.logical_not(home))
    def _():
        s1_near.start()

    @pl.when(home)
    def _():
        s1_local.start()

    w_send_first(True)
    for c in range(CHUNKS):
        for here, there in w_lanes(c):
            pltpu.make_async_copy(w_ref.at[:, here], wg.at[0, c, :, there], local_sem.at[3]).start()

    h = ext[:rows, :].astype(F32)
    squares = h * h

    def total_lanes(v):
        acc = v[:, :128]
        for k in range(128, v.shape[1], 128):
            acc = acc + v[:, k : k + 128]
        return jnp.broadcast_to(jnp.sum(acc.T, axis=0, keepdims=True), (8, rows))

    def spread(row):
        return jnp.broadcast_to(row, (128, rows)).T

    def reduce_start(base, v):
        small[base] = v
        c = copy(small.at[base], small.at[base + 1], sm_s.at[base], sm_r.at[base + 1], at(core_=other))
        c.start()

    def reduce_zl(base):
        copy(small.at[base], small.at[base + 1], sm_s.at[base], sm_r.at[base + 1], at(core_=other)).wait()
        small[base + 2] = small[base] + small[base + 1]
        copy(small.at[base + 2], small.at[base + 3], sm_s.at[base + 2], sm_r.at[base + 3], at(zl_=1 - zl)).start()

    def reduce_y_copies(base):
        return [
            copy(
                small.at[base + 4], small.at[base + 4 + k], sm_s.at[base + 4 + k], sm_r.at[base + 4 + k],
                at(y_=rotate(y, k, NY)),
            )
            for k in (1, 2, 3)
        ]

    def reduce_y(base):
        copy(small.at[base + 2], small.at[base + 3], sm_s.at[base + 2], sm_r.at[base + 3], at(zl_=1 - zl)).wait()
        small[base + 4] = small[base + 2] + small[base + 3]
        for c in reduce_y_copies(base):
            c.start()

    def reduce_end(base):
        for c in reduce_y_copies(base):
            c.wait()
        return (small[base + 4] + small[base + 5]) + (small[base + 6] + small[base + 7])

    reduce_start(0, total_lanes(squares))

    cut = 9 * 16
    parts = (pl.ds(0, cut), pl.ds(cut, raw.shape[2] - cut))

    def s2_direct(half, up):
        to = at(y_=rotate(y, 1 if up else 3, NY))
        piece = raw.at[half, y]
        return copy(piece, piece, s2_s.at[0], s2_r.at[half, int(up)], to)

    def s2_arrival(half, up):
        to = at(y_=rotate(y, 1 if up else 3, NY))
        piece = raw.at[half, rotate(y, 3 if up else 1, NY)]
        return copy(piece, piece, s2_s.at[0], s2_r.at[half, int(up)], to)

    def s2_forward(half, up):
        to = at(y_=rotate(y, 1 if up else 3, NY))
        piece = raw.at[half, rotate(y, 3 if up else 1, NY), parts[0 if up else 1]]
        return copy(piece, piece, s2f_s.at[0], s2f_r.at[half, int(up)], to)

    def s2_last(half, up):
        to = at(y_=rotate(y, 1 if up else 3, NY))
        piece = raw.at[half, rotate(y, 2, NY), parts[0 if up else 1]]
        return copy(piece, piece, s2f_s.at[0], s2f_r.at[half, int(up)], to)

    def s3_copy(half, k):
        piece = a.at[core + 2 * half, rotate(y, 4 - k, NY)]
        return copy(piece, piece, s3_s.at[0], s3_r.at[0], at(core_=other))

    def s3_all():
        pieces = a.at[pl.ds(0, 2)]
        return copy(pieces, pieces, s3_s.at[0], s3_r.at[0], at(core_=other))

    def normalise(half, k):
        s = rotate(y, 4 - k, NY)
        g = raw[half, s, rows : rows + 16, :].astype(F32)[:1]
        v = raw[half, s, :rows, :].astype(F32) * wide(piece_inv[half]) * g
        a[core + 2 * half, s] = v.astype(BF16)
        s3_copy(half, k).start()

    def wide(v):
        return jnp.concatenate([v] * (feats // 128), axis=1)

    def inverse(row):
        return 1.0 / jnp.sqrt(spread(row) / width + EPS)

    def xt_copy(k):
        return copy(xtot.at[x], xtot.at[x], xt_s.at[k - 1], xt_r.at[k - 1], at(x_=rotate(x, k, NX)))

    def xt_arrival(k):
        piece = xtot.at[rotate(x, 4 - k, NX)]
        return copy(piece, piece, xt_s.at[k - 1], xt_r.at[k - 1], at(x_=rotate(x, k, NX)))

    reduce_zl(0)
    s1_far.wait_send()
    w_send_first(False)
    reduce_y(0)
    for half in (0, 1):
        copy(ext, raw.at[half, y], s1_s.at[0], s1_r.at[half], at(core_=other)).wait_recv()
        for up in (True, False):
            s2_direct(half, up).start()
    w_send(1)
    xtot[x] = reduce_end(0)
    for k in (1, 2, 3):
        xt_copy(k).start()
    hop(0, 0)
    for k in (1, 2, 3):
        xt_arrival(k).wait_recv()
    inv_ref[...] = inverse(xtot[x][:1])
    for half in (0, 1):
        piece_inv[half] = inverse(xtot[core + 2 * half][:1])
    racc[...] = jnp.zeros_like(racc)
    for half in (0, 1):
        normalise(half, 0)
    hop(0, 1)
    for half in (0, 1):
        for up in (True, False):
            s2_arrival(half, up).wait_recv()
            s2_forward(half, up).start()
    hop(1, 0)
    w_send(2)
    for half in (0, 1):
        for k in (1, 3):
            normalise(half, k)
    hop(1, 1)
    for half in (0, 1):
        for up in (True, False):
            s2_last(half, up).wait_recv()
        normalise(half, 2)
    hop(2, 0)
    load_len.wait()
    load_q.wait()
    load_og.wait()
    pltpu.make_async_copy(wg.at[0], wg.at[0], local_sem.at[3]).wait()
    s3_all().wait_recv()
    hop(0, 2)
    hop(2, 1)

    def sequence(b):
        return pl.ds(pl.multiple_of(b * src, src), src)

    def rs_copy(c, j, b):
        part = sequence(b)
        return copy(
            part_send.at[c, j, part], rs_recv.at[c, j, part], rs_s.at[0], rs_r.at[c, b],
            at(x_=rotate(x, 1 + j, NX)),
        )

    def rs_arrived(c, b):
        pieces = rs_recv.at[c, :, sequence(b)]
        copy(pieces, pieces, rs_s.at[0], rs_r.at[c, b], at(core_=other)).wait_recv()

    def ag_copy(c, j, b):
        piece = ag.at[c, x, sequence(b)]
        return copy(piece, piece, ag_s.at[0], ag_r.at[c, b], at(x_=rotate(x, 1 + j, NX)))

    def ag_arrived(c, b):
        pieces = ag.at[c, pl.ds(0, 3), sequence(b)]
        copy(pieces, pieces, ag_s.at[0], ag_r.at[c, b], at(core_=other)).wait_recv()

    def project(c):
        for up in (True, False):
            w_copy(4, c, up).wait_recv()
            w_copy(3, c, up).wait_recv()

        def one(j, b):
            xs = rotate(x, 1 + j, NX)
            acc = jnp.zeros((src, cols), F32)
            for r in range(4):
                acc = acc + jnp.dot(a[xs, rotate(zh, r, NZ), sequence(b), :], wg[r, c], preferred_element_type=F32)
            return acc

        def sequences(b, carry):
            for j in (1, 0, 2):
                part_send[c, j, sequence(b), :] = one(j, b).astype(BF16)
                rs_copy(c, j, b).start()
            own_part[c, sequence(b), :] = one(3, b)
            return carry

        lax.fori_loop(0, batches, sequences, 0)

    lane = lax.broadcasted_iota(jnp.int32, (1, 128), 1)
    first = lane < HEAD_DIM
    place = lax.rem(lax.broadcasted_iota(jnp.int32, (1, 2 * src), 1), src)

    def two_heads(v):
        return jnp.concatenate([jnp.where(first, v, 0.0), jnp.where(first, 0.0, v)], axis=0).astype(BF16)

    def per_head(v, f):
        return jnp.concatenate([f(v[:, :src]), f(v[:, src:])], axis=1)

    def dot_t(m, n):
        return lax.dot_general(m, n, (((1,), (1,)), ((), ())), preferred_element_type=F32)

    def t_dot(m, n):
        return lax.dot_general(m, n, (((0,), (0,)), ((), ())), preferred_element_type=F32)

    def attend(c):
        lanes = pl.ds(pl.multiple_of(c * 128, 128), 128)

        def one(b, carry):
            at_rows = sequence(b)
            kv_b = own_part[c, at_rows, :]
            rs_arrived(c, b)
            for j in range(3):
                kv_b = kv_b + rs_recv[c, j, at_rows, :].astype(F32)
            keys = two_heads(kv_b[:, :128].astype(BF16).astype(F32))
            values = two_heads(kv_b[:, 128:].astype(BF16).astype(F32))
            query, cotan = q_ref[b, :, lanes], og_ref[b, :, lanes]
            expo = jnp.where(place < len_ref[b], jnp.exp(dot_t(query, keys) * SCALE), 0.0)
            probs = per_head(expo, lambda e: e / jnp.sum(e, axis=-1, keepdims=True))
            probs_b = probs.astype(BF16)
            att_ref[b, :, lanes] = jnp.dot(probs_b, values, preferred_element_type=F32).astype(BF16)
            dprob = dot_t(cotan, values)
            delta = per_head(
                probs * dprob, lambda e: jnp.broadcast_to(jnp.sum(e, axis=-1, keepdims=True), e.shape)
            )
            dscore = (probs * (dprob - delta) * SCALE).astype(BF16)
            gq_ref[b, :, lanes] = jnp.dot(dscore, keys, preferred_element_type=F32).astype(BF16)
            dkey, dvalue = t_dot(dscore, query), t_dot(probs_b, cotan)
            dkv = jnp.concatenate(
                [jnp.where(first, dkey[:src], dkey[src:]), jnp.where(first, dvalue[:src], dvalue[src:])], axis=1
            ).astype(BF16)
            ag[c, x, at_rows, :] = dkv
            for j in (1, 0, 2):
                ag_copy(c, j, b).start()
            product = dkv.astype(F32) * kv_b
            racc[at_rows, :] = racc[at_rows, :] + (product[:, :128] + product[:, 128:])
            return carry

        lax.fori_loop(0, batches, one, 0)

    def back(chunks):
        for c in chunks:
            for b in range(batches):
                ag_arrived(c, b)

        def one(r, carry):
            term = dot_t(ag[chunks[0]].reshape(4 * rows, cols), wg[r, chunks[0]])
            for c in chunks[1:]:
                term = term + dot_t(ag[c].reshape(4 * rows, cols), wg[r, c])
            for xs in range(4):
                mine = term[xs * rows : (xs + 1) * rows]
                dn[xs, r] = mine if chunks[0] == 0 else dn[xs, r] + mine
            return carry

        lax.fori_loop(0, 4, one, 0)

    project(0)
    hop(1, 2)
    w_send(3)
    project(1)
    attend(0)
    hop(2, 2)
    attend(1)
    hop(0, 3)
    back((0,))
    project(2)
    hop(1, 3)
    back((1,))
    hop(2, 3)
    attend(2)
    project(3)
    attend(3)
    reduce_start(8, total_lanes(racc[...]))
    last = CHUNKS - 1
    for r in range(4):
        turned[r] = wg[r, last].T
    back((2,))

    SHARES = ((0, src), (src, src // 2), (src + src // 2, src - src // 2))

    def share(b):
        return pl.ds(*SHARES[b])

    def d1_copy(b, half, k):
        part = share(b)
        return copy(
            core_send.at[half, k, part], core_recv.at[half, k, part],
            d1_s.at[0], d1_r.at[b, half, k], at(core_=other),
        )

    SLOT = {1: 0, 3: 1, 2: 2}

    def d2_copy(b, half, k):
        part, slot, two = share(b), SLOT[k], int(k == 2)
        return copy(
            y_send.at[half, slot, part], y_recv.at[half, slot, part], d2_s.at[two], d2_r.at[two, b],
            at(y_=rotate(y, k, NY)),
        )

    def d2_arrived(b):
        pieces = y_recv.at[:, pl.ds(0, 2), share(b)]
        copy(pieces, pieces, d2_s.at[0], d2_r.at[0, b], at(core_=other)).wait_recv()
        d2_copy(b, 0, 2).wait_recv()

    def whole(b, xs, k):
        part = share(b)
        r = lax.rem(y + k + NZ - zh, NZ)
        return dn[xs, r, part, :] + jnp.dot(ag[last, xs, part, :], turned[r], preferred_element_type=F32)

    def dz_copy(b):
        part = share(b)
        return copy(z_send.at[part], z_recv.at[part], dz_s.at[b], dz_r.at[b], at(zl_=1 - zl))

    def chip_sum(b, half, k):
        v = whole(b, core + 2 * half, k)
        d1_copy(b, half, k).wait_recv()
        return v + core_recv[half, k, share(b), :].astype(F32)

    def cores(b):
        if b < batches:
            ag_arrived(last, b)
        part = share(b)
        for k in (2, 1, 3, 0):
            for half in (0, 1):
                core_send[half, k, part, :] = whole(b, other + 2 * half, k).astype(BF16)
                d1_copy(b, half, k).start()
        z_send[part, :] = chip_sum(b, 1 - zl, 2).astype(BF16)
        dz_copy(b).start()

    def one_step(b):
        for half in (0, 1):
            for k in (1, 3):
                y_send[half, SLOT[k], share(b), :] = chip_sum(b, half, k).astype(BF16)
                d2_copy(b, half, k).start()

    def two_steps(b):
        part = share(b)
        v = chip_sum(b, zl, 2)
        dz_copy(b).wait_recv()
        y_send[0, 2, part, :] = (v + z_recv[part, :].astype(F32)).astype(BF16)
        d2_copy(b, 0, 2).start()

    cores(0)
    one_step(0)
    reduce_zl(8)
    cores(1)
    two_steps(0)
    reduce_y(8)
    one_step(1)
    cores(2)
    two_steps(1)
    one_step(2)
    two_steps(2)
    for b in range(3):
        for half in (0, 1):
            y_own[half, share(b), :] = chip_sum(b, half, 0)

    def d3_copy(b, half):
        part = share(b)
        to = (y, zh * 4 + core + 2 * half, x)
        return copy(fin_send.at[half, part], fin.at[zl, part], d3_s.at[b, half], d3_r.at[b, zl], to)

    def stays(half):
        return jnp.logical_and(home, x // 2 == half)

    def deliver(b):
        part = share(b)
        d2_arrived(b)
        for half in (0, 1):
            v = y_own[half, part, :]
            for k in (1, 3):
                v = v + y_recv[half, SLOT[k], part, :].astype(F32)
            v = v + jnp.where(zl == half, y_recv[0, 2, part, :].astype(F32), 0.0)
            fin_send[half, part, :] = v.astype(BF16)

            @pl.when(stays(half))
            def _():
                pltpu.make_async_copy(fin_send.at[half, part], fin.at[zl, part], d3_r.at[b, zl]).start()

            @pl.when(jnp.logical_not(stays(half)))
            def _():
                d3_copy(b, half).start()

    def weighed(v, half, k):
        hidden = raw[half, rotate(y, k, NY), :rows, :].astype(F32) * wide(piece_inv[half])
        return jnp.sum(v.astype(F32) * hidden, axis=0, keepdims=True)

    def folded(v):
        lanes = [v[:, i : i + 128] for i in range(0, feats, 128)]
        return jnp.concatenate(lanes + lanes, axis=0)

    def gz_copy(k):
        return copy(gz.at[zh], gz.at[zh], gz_s.at[k - 1], gz_r.at[k - 1], at(zh_=rotate(zh, k, NZ)))

    def gz_arrival(k):
        piece = gz.at[rotate(zh, 4 - k, NZ)]
        return copy(piece, piece, gz_s.at[k - 1], gz_r.at[k - 1], at(zh_=rotate(zh, k, NZ)))

    def gy_copy(k):
        return copy(gz.at[4, k], gy.at[y], gy_s.at[k - 1], gy_r.at[k - 1], at(y_=rotate(y, k, NY)))

    def gy_arrival(k):
        piece = gy.at[rotate(y, 4 - k, NY)]
        return copy(piece, piece, gy_s.at[k - 1], gy_r.at[k - 1], at(y_=rotate(y, k, NY)))

    def gx_copy(x_):
        place = 2 * zl + core
        return copy(gy.at[4], gx.at[place], gx_s.at[x_], gx_r.at[place], (y, zh * 4 + x_, x))

    gz[zh, 0] = folded(weighed(y_own[0], 0, 0) + weighed(y_own[1], 1, 0))
    for k in (1, 3):
        gz[zh, k] = folded(weighed(y_send[0, SLOT[k]], 0, k) + weighed(y_send[1, SLOT[k]], 1, k))
    gz[zh, 2] = folded(weighed(y_send[0, 2], zl, 2))
    for k in (1, 2, 3):
        gz_copy(k).start()
    deliver(0)
    inv = inv_ref[...]
    rsum_ref[...] = spread(reduce_end(8)[:1]) * inv * inv / width
    for k in (1, 2, 3):
        gz_arrival(k).wait_recv()
    gz[4] = (gz[0] + gz[1]) + (gz[2] + gz[3])
    gy[y] = gz[4, 0]
    for k in (1, 2, 3):
        gy_copy(k).start()

    def all_sent(pieces, sem, arrived):
        copy(pieces, pieces, sem, arrived, at(core_=other)).wait_send()

    all_sent(through, w_s.at[0], w_r.at[0, 0, 0])
    for stage in range(1, 5):
        all_sent(through_half, w_s.at[stage], w_r.at[stage, 0, 0])
    all_sent(part_send, rs_s.at[0], rs_r.at[0, 0])
    all_sent(ag.at[:, pl.ds(0, 3)], ag_s.at[0], ag_r.at[0, 0])
    all_sent(raw.at[0], s2_s.at[0], s2_r.at[0, 0])
    all_sent(raw.at[0, pl.ds(0, 2)], s2f_s.at[0], s2f_r.at[0, 0])
    s3_all().wait_send()
    all_sent(core_send, d1_s.at[0], d1_r.at[0, 0, 0])

    @pl.when(jnp.logical_not(home))
    def _():
        s1_near.wait_send()

    for k in (1, 2, 3):
        xt_copy(k).wait_send()
    deliver(1)
    deliver(2)

    def owned(b):
        part = share(b)
        for k in (0, 1):
            copy(fin_send.at[0, part], fin.at[k, part], d3_s.at[b, 0], d3_r.at[b, k], at(core_=other)).wait_recv()
        dnormed = fin[0, part, :].astype(F32) + fin[1, part, :].astype(F32)
        own_gain = ext[rows : rows + 16, :].astype(F32)[:1]
        gs_ref[part, :] = own_gain * (wide(inv_ref[part, :]) * dnormed) - ext[part, :].astype(F32) * wide(
            rsum_ref[part, :]
        )

    for k in (1, 2, 3):
        gy_arrival(k).wait_recv()
    gy[4] = (gy[0] + gy[1]) + (gy[2] + gy[3])
    for x_ in range(NX):
        itself = jnp.logical_and(home, x == x_)

        @pl.when(itself)
        def _():
            place = 2 * zl + core
            pltpu.make_async_copy(gy.at[4], gx.at[place], gx_r.at[place]).start()

        @pl.when(jnp.logical_not(itself))
        def _():
            gx_copy(x_).start()

    owned(0)
    owned(1)
    owned(2)

    all_sent(y_send.at[:, pl.ds(0, 2)], d2_s.at[0], d2_r.at[0, 0])
    all_sent(y_send.at[0, 2], d2_s.at[1], d2_r.at[1, 0])
    for b in range(3):
        dz_copy(b).wait_send()
        for half in (0, 1):

            @pl.when(jnp.logical_not(stays(half)))
            def _():
                d3_copy(b, half).wait_send()

    for k in (1, 2, 3):
        gz_copy(k).wait_send()
        gy_copy(k).wait_send()
    for x_ in range(NX):

        @pl.when(jnp.logical_not(jnp.logical_and(home, x == x_)))
        def _():
            gx_copy(x_).wait_send()

    for k in range(4):
        copy(gy.at[4], gx.at[k], gx_s.at[0], gx_r.at[k], at(core_=other)).wait_recv()
    total = (gx[0] + gx[1]) + (gx[2] + gx[3])
    gg_ref[...] = jnp.concatenate([total[i : i + 1] for i in range(feats // 128)], axis=1)


def per_device(states, gain, kv_weight, queries, out_grad, src_len):
    batches, src, feats = states.shape
    tgt, heads_cols = queries.shape[2:]
    rows = batches * src
    cols = 2 * heads_cols // CHUNKS
    w = kv_weight.reshape(feats, 2 * heads_cols)
    gains = jnp.broadcast_to(gain[None, :], (16, feats))
    vmem = pl.BlockSpec(memory_space=pltpu.VMEM)
    dma = pltpu.SemaphoreType.DMA
    out = pl.pallas_call(
        kernel,
        out_shape=(
            jax.ShapeDtypeStruct((batches, tgt, heads_cols), BF16),
            jax.ShapeDtypeStruct((batches, tgt, heads_cols), BF16),
            jax.ShapeDtypeStruct((rows, feats), F32),
            jax.ShapeDtypeStruct((1, feats), F32),
        ),
        in_specs=[pl.BlockSpec(memory_space=pl.ANY)] * 6,
        out_specs=[vmem] * 4,
        scratch_shapes=[
            pltpu.SMEM((batches,), jnp.int32),
            pltpu.VMEM((rows + 16, feats), BF16),
            pltpu.VMEM((batches, tgt, heads_cols), BF16),
            pltpu.VMEM((batches, tgt, heads_cols), BF16),
            pltpu.VMEM((4, CHUNKS, feats, cols), BF16),
            pltpu.VMEM((2, CHUNKS, feats, cols), BF16),
            pltpu.VMEM((2, CHUNKS, feats // 2, cols), BF16),
            pltpu.VMEM((4, cols, feats), BF16),
            pltpu.VMEM((2, 4, rows + 16, feats), BF16),
            pltpu.VMEM((4, 4, rows, feats), BF16),
            pltpu.VMEM((CHUNKS, rows, cols), F32),
            pltpu.VMEM((CHUNKS, 3, rows, cols), BF16),
            pltpu.VMEM((CHUNKS, 3, rows, cols), BF16),
            pltpu.VMEM((CHUNKS, 4, rows, cols), BF16),
            pltpu.VMEM((4, 4, rows, feats), F32),
            pltpu.VMEM((2, 4, rows, feats), BF16),
            pltpu.VMEM((2, 4, rows, feats), BF16),
            pltpu.VMEM((rows, feats), BF16),
            pltpu.VMEM((rows, feats), BF16),
            pltpu.VMEM((2, 3, rows, feats), BF16),
            pltpu.VMEM((2, 3, rows, feats), BF16),
            pltpu.VMEM((2, rows, feats), F32),
            pltpu.VMEM((2, rows, feats), BF16),
            pltpu.VMEM((2, rows, feats), BF16),
            pltpu.VMEM((rows, 128), F32),
            pltpu.VMEM((16, 8, rows), F32),
            pltpu.VMEM((4, 8, rows), F32),
            pltpu.VMEM((5, 4, 8, 128), F32),
            pltpu.VMEM((5, 8, 128), F32),
            pltpu.VMEM((4, 8, 128), F32),
            pltpu.VMEM((rows, 128), F32),
            pltpu.VMEM((2, rows, 128), F32),
            pltpu.VMEM((rows, 128), F32),
            dma((6,)),
            dma((5,)), dma((5, 2, CHUNKS)),
            dma((2,)), dma((2,)),
            dma((1,)), dma((2, 2)), dma((1,)), dma((2, 2)),
            dma((1,)), dma((1,)),
            dma((1,)), dma((CHUNKS, 2)),
            dma((1,)), dma((CHUNKS, 2)),
            dma((1,)), dma((3, 2, 4)),
            dma((3,)), dma((3,)),
            dma((2,)), dma((2, 3)),
            dma((3, 2)), dma((3, 2)),
            dma((16,)), dma((16,)),
            dma((3,)), dma((3,)),
            dma((3,)), dma((3,)),
            dma((3,)), dma((3,)),
            dma((4,)), dma((4,)),
        ],
        compiler_params=pltpu.CompilerParams(
            collective_id=1, has_side_effects=True, vmem_limit_bytes=52 * 2**20
        ),
        name="cross_attention",
    )(
        w, states.reshape(rows, feats), gains, queries[0], out_grad[0], src_len
    )
    attended, grad_q, grad_states, grad_gain = out
    return attended[None], grad_q[None], grad_states.reshape(batches, src, feats), grad_gain[0]


def solution(mesh):
    return jax.shard_map(
        per_device,
        mesh=mesh,
        in_specs=(
            P("dp", None, ("section", "tensor")),
            P(("section", "tensor")),
            P("section", "dp", None, "tensor"),
            P("section", "dp", None, "tensor"),
            P("section", "dp", None, "tensor"),
            P("dp"),
        ),
        out_specs=(
            P("section", "dp", None, "tensor"),
            P("section", "dp", None, "tensor"),
            P("dp", None, ("section", "tensor")),
            P(("section", "tensor")),
        ),
        check_vma=False,
    )
```

```python
import jax
import jax.numpy as jnp
from jax import lax
from jax.experimental import pallas as pl
from jax.experimental.pallas import tpu as pltpu
from jax.sharding import PartitionSpec as P

MESH = pl.DeviceIdType.MESH
HEAD_DIM = 64
SCALE = HEAD_DIM ** (-0.5)
EPS = 1e-06
NX, NY, NZ = 4, 4, 4
CHUNKS = 4
F32, BF16 = jnp.float32, jnp.bfloat16


def rotate(a, by, n):
    return lax.rem(a + by, n)


def kernel(
    w_ref, states_in, gain_in, q_in, og_in, len_in,
    att_ref, gq_ref, gs_ref, gg_ref,
    len_ref, ext, q_ref, og_ref, wg, through, through_half, turned, raw, a, own_part, part_send, rs_recv, ag, dn, core_send, core_recv, z_send, z_recv, y_send, y_recv,
    y_own, fin_send, fin, racc, small, xtot, gz, gy, gx, inv_ref, piece_inv, rsum_ref,
    local_sem, w_s, w_r, s1_s, s1_r, s2_s, s2_r, s2f_s, s2f_r, s3_s, s3_r, rs_s, rs_r, ag_s, ag_r,
    d1_s, d1_r, dz_s, dz_r, d2_s, d2_r, d3_s, d3_r, sm_s, sm_r, xt_s, xt_r, gz_s, gz_r, gy_s, gy_r, gx_s, gx_r,
):
    y, d, t = lax.axis_index("section"), lax.axis_index("dp"), lax.axis_index("tensor")
    zh, x, zl, core = d // 4, lax.rem(d, 4), t // 2, lax.rem(t, 2)
    rows, feats = gs_ref.shape
    batches = q_ref.shape[0]
    src = rows // batches
    cols = wg.shape[3]
    heads_cols = q_ref.shape[2]
    width = NX * NZ * feats

    def at(y_=None, zh_=None, x_=None, zl_=None, core_=None):
        pick = lambda new, old: old if new is None else new
        return (pick(y_, y), pick(zh_, zh) * 4 + pick(x_, x), pick(zl_, zl) * 2 + pick(core_, core))

    def copy(src_ref, dst_ref, send, recv, to):
        return pltpu.make_async_remote_copy(
            src_ref=src_ref, dst_ref=dst_ref, send_sem=send, recv_sem=recv, device_id=to, device_id_type=MESH
        )

    other = 1 - core
    home = t == x

    load_ext = pltpu.make_async_copy(states_in, ext.at[:rows], local_sem.at[0])
    load_gain = pltpu.make_async_copy(gain_in, ext.at[rows : rows + 16], local_sem.at[4])
    load_len = pltpu.make_async_copy(len_in, len_ref, local_sem.at[5])
    load_q = pltpu.make_async_copy(q_in, q_ref, local_sem.at[1])
    load_og = pltpu.make_async_copy(og_in, og_ref, local_sem.at[2])
    load_ext.start()
    load_gain.start()
    load_len.start()
    load_q.start()
    load_og.start()
    barrier = pltpu.get_barrier_semaphore()

    def greet(to):
        pl.semaphore_signal(barrier, inc=1, device_id=to, device_id_type=MESH)

    for k in (1, 2, 3):
        greet(at(zh_=rotate(zh, k, NZ)))
        greet(at(y_=rotate(y, k, NY)))
        greet(at(x_=rotate(x, k, NX)))
    greet(at(core_=other))
    above = at(zh_=rotate(zh, zl, NZ), zl_=1 - zl)
    below = at(zh_=rotate(zh, 3 + zl, NZ), zl_=1 - zl)
    greet(above)
    greet(below)
    for zl_ in (0, 1):
        for core_ in (0, 1):
            itself = jnp.logical_and(home, jnp.logical_and(zl == zl_, core == core_))

            @pl.when(jnp.logical_not(itself))
            def _():
                greet(at(x_=t, zl_=zl_, core_=core_))

    for x_ in range(NX):

        @pl.when(jnp.logical_not(jnp.logical_and(home, x == x_)))
        def _():
            greet((y, zh * 4 + x_, x))

    @pl.when(jnp.logical_not(home))
    def _():
        pl.semaphore_wait(barrier, 20)

    @pl.when(home)
    def _():
        pl.semaphore_wait(barrier, 18)

    x_core = lax.rem(x, 2)

    def w_lanes(c):
        k = pl.ds(pl.multiple_of(c * 128, 128), 128)
        v = pl.ds(pl.multiple_of(heads_cols + c * 128, 128), 128)
        return ((k, pl.ds(0, 128)), (v, pl.ds(128, 128)))

    def w_copy(stage, c, up):
        half = feats // 2
        part, rest = pl.ds(0 if up else half, half), pl.ds(half if up else 0, half)
        way, direct = int(up), wg.at[3 if up else 1, c]
        here, there = (
            (through.at[way, c], through.at[way, c]),
            (through.at[way, c, part], direct.at[part]),
            (direct.at[part], through_half.at[way, c]),
            (through_half.at[way, c], wg.at[2, c, part]),
            (through.at[way, c, rest], direct.at[rest]),
        )[stage]
        return copy(here, there, w_s.at[stage], w_r.at[stage, way, c], above if up else below)

    def w_send_way(c, up):
        for here, there in w_lanes(c):
            copy(
                w_ref.at[:, here], through.at[int(up), c, :, there],
                w_s.at[0], w_r.at[0, int(up), c], above if up else below,
            ).start()

    def w_send(c):
        for up in (True, False):
            w_send_way(c, up)

    def w_send_first(outward):
        for up in (True, False):

            @pl.when((zl == int(up)) if outward else (zl != int(up)))
            def _():
                w_send_way(0, up)

    def hop(stage, c):
        for up in (True, False):
            w_copy(stage, c, up).wait_recv()
            w_copy(stage + 1, c, up).start()
            if stage == 0:
                w_copy(4, c, up).start()

    load_ext.wait()
    load_gain.wait()

    def s1_copy(z, to):
        return copy(ext, raw.at[x // 2, y], s1_s.at[z], s1_r.at[x // 2], to)

    s1_far = s1_copy(1, at(x_=t, zl_=1 - zl, core_=x_core))
    s1_near = s1_copy(0, at(x_=t, core_=x_core))
    s1_local = pltpu.make_async_copy(ext, raw.at[x // 2, y], s1_r.at[x // 2])
    s1_far.start()

    @pl.when(jnp.logical_not(home))
    def _():
        s1_near.start()

    @pl.when(home)
    def _():
        s1_local.start()

    w_send_first(True)
    for c in range(CHUNKS):
        for here, there in w_lanes(c):
            pltpu.make_async_copy(w_ref.at[:, here], wg.at[0, c, :, there], local_sem.at[3]).start()

    h = ext[:rows, :].astype(F32)
    squares = h * h

    def total_lanes(v):
        acc = v[:, :128]
        for k in range(128, v.shape[1], 128):
            acc = acc + v[:, k : k + 128]
        return jnp.broadcast_to(jnp.sum(acc.T, axis=0, keepdims=True), (8, rows))

    def spread(row):
        return jnp.broadcast_to(row, (128, rows)).T

    def reduce_start(base, v):
        small[base] = v
        c = copy(small.at[base], small.at[base + 1], sm_s.at[base], sm_r.at[base + 1], at(core_=other))
        c.start()

    def reduce_zl(base):
        copy(small.at[base], small.at[base + 1], sm_s.at[base], sm_r.at[base + 1], at(core_=other)).wait()
        small[base + 2] = small[base] + small[base + 1]
        copy(small.at[base + 2], small.at[base + 3], sm_s.at[base + 2], sm_r.at[base + 3], at(zl_=1 - zl)).start()

    def reduce_y_copies(base):
        return [
            copy(
                small.at[base + 4], small.at[base + 4 + k], sm_s.at[base + 4 + k], sm_r.at[base + 4 + k],
                at(y_=rotate(y, k, NY)),
            )
            for k in (1, 2, 3)
        ]

    def reduce_y(base):
        copy(small.at[base + 2], small.at[base + 3], sm_s.at[base + 2], sm_r.at[base + 3], at(zl_=1 - zl)).wait()
        small[base + 4] = small[base + 2] + small[base + 3]
        for c in reduce_y_copies(base):
            c.start()

    def reduce_end(base):
        for c in reduce_y_copies(base):
            c.wait()
        return (small[base + 4] + small[base + 5]) + (small[base + 6] + small[base + 7])

    reduce_start(0, total_lanes(squares))

    cut = 9 * 16
    parts = (pl.ds(0, cut), pl.ds(cut, raw.shape[2] - cut))

    def s2_direct(half, up):
        to = at(y_=rotate(y, 1 if up else 3, NY))
        piece = raw.at[half, y]
        return copy(piece, piece, s2_s.at[0], s2_r.at[half, int(up)], to)

    def s2_arrival(half, up):
        to = at(y_=rotate(y, 1 if up else 3, NY))
        piece = raw.at[half, rotate(y, 3 if up else 1, NY)]
        return copy(piece, piece, s2_s.at[0], s2_r.at[half, int(up)], to)

    def s2_forward(half, up):
        to = at(y_=rotate(y, 1 if up else 3, NY))
        piece = raw.at[half, rotate(y, 3 if up else 1, NY), parts[0 if up else 1]]
        return copy(piece, piece, s2f_s.at[0], s2f_r.at[half, int(up)], to)

    def s2_last(half, up):
        to = at(y_=rotate(y, 1 if up else 3, NY))
        piece = raw.at[half, rotate(y, 2, NY), parts[0 if up else 1]]
        return copy(piece, piece, s2f_s.at[0], s2f_r.at[half, int(up)], to)

    def s3_copy(half, k):
        piece = a.at[core + 2 * half, rotate(y, 4 - k, NY)]
        return copy(piece, piece, s3_s.at[0], s3_r.at[0], at(core_=other))

    def s3_all():
        pieces = a.at[pl.ds(0, 2)]
        return copy(pieces, pieces, s3_s.at[0], s3_r.at[0], at(core_=other))

    def normalise(half, k):
        s = rotate(y, 4 - k, NY)
        g = raw[half, s, rows : rows + 16, :].astype(F32)[:1]
        v = raw[half, s, :rows, :].astype(F32) * wide(piece_inv[half]) * g
        a[core + 2 * half, s] = v.astype(BF16)
        s3_copy(half, k).start()

    def wide(v):
        return jnp.concatenate([v] * (feats // 128), axis=1)

    def inverse(row):
        return 1.0 / jnp.sqrt(spread(row) / width + EPS)

    def xt_copy(k):
        return copy(xtot.at[x], xtot.at[x], xt_s.at[k - 1], xt_r.at[k - 1], at(x_=rotate(x, k, NX)))

    def xt_arrival(k):
        piece = xtot.at[rotate(x, 4 - k, NX)]
        return copy(piece, piece, xt_s.at[k - 1], xt_r.at[k - 1], at(x_=rotate(x, k, NX)))

    reduce_zl(0)
    s1_far.wait_send()
    w_send_first(False)
    reduce_y(0)
    for half in (0, 1):
        copy(ext, raw.at[half, y], s1_s.at[0], s1_r.at[half], at(core_=other)).wait_recv()
        for up in (True, False):
            s2_direct(half, up).start()
    w_send(1)
    xtot[x] = reduce_end(0)
    for k in (1, 2, 3):
        xt_copy(k).start()
    hop(0, 0)
    for k in (1, 2, 3):
        xt_arrival(k).wait_recv()
    inv_ref[...] = inverse(xtot[x][:1])
    for half in (0, 1):
        piece_inv[half] = inverse(xtot[core + 2 * half][:1])
    racc[...] = jnp.zeros_like(racc)
    for half in (0, 1):
        normalise(half, 0)
    hop(0, 1)
    for half in (0, 1):
        for up in (True, False):
            s2_arrival(half, up).wait_recv()
            s2_forward(half, up).start()
    hop(1, 0)
    w_send(2)
    for half in (0, 1):
        for k in (1, 3):
            normalise(half, k)
    hop(1, 1)
    for half in (0, 1):
        for up in (True, False):
            s2_last(half, up).wait_recv()
        normalise(half, 2)
    hop(2, 0)
    load_len.wait()
    load_q.wait()
    load_og.wait()
    pltpu.make_async_copy(wg.at[0], wg.at[0], local_sem.at[3]).wait()
    s3_all().wait_recv()
    hop(0, 2)
    hop(2, 1)

    def sequence(b):
        return pl.ds(pl.multiple_of(b * src, src), src)

    def rs_copy(c, j, b):
        part = sequence(b)
        return copy(
            part_send.at[c, j, part], rs_recv.at[c, j, part], rs_s.at[0], rs_r.at[c, b],
            at(x_=rotate(x, 1 + j, NX)),
        )

    def rs_arrived(c, b):
        pieces = rs_recv.at[c, :, sequence(b)]
        copy(pieces, pieces, rs_s.at[0], rs_r.at[c, b], at(core_=other)).wait_recv()

    def ag_copy(c, j, b):
        piece = ag.at[c, x, sequence(b)]
        return copy(piece, piece, ag_s.at[0], ag_r.at[c, b], at(x_=rotate(x, 1 + j, NX)))

    def ag_arrived(c, b):
        pieces = ag.at[c, pl.ds(0, 3), sequence(b)]
        copy(pieces, pieces, ag_s.at[0], ag_r.at[c, b], at(core_=other)).wait_recv()

    def project(c):
        for up in (True, False):
            w_copy(4, c, up).wait_recv()
            w_copy(3, c, up).wait_recv()

        def one(j, b):
            xs = rotate(x, 1 + j, NX)
            acc = jnp.zeros((src, cols), F32)
            for r in range(4):
                acc = acc + jnp.dot(a[xs, rotate(zh, r, NZ), sequence(b), :], wg[r, c], preferred_element_type=F32)
            return acc

        def sequences(b, carry):
            for j in (1, 0, 2):
                part_send[c, j, sequence(b), :] = one(j, b).astype(BF16)
                rs_copy(c, j, b).start()
            own_part[c, sequence(b), :] = one(3, b)
            return carry

        lax.fori_loop(0, batches, sequences, 0)

    lane = lax.broadcasted_iota(jnp.int32, (1, 128), 1)
    first = lane < HEAD_DIM
    place = lax.rem(lax.broadcasted_iota(jnp.int32, (1, 2 * src), 1), src)

    def two_heads(v):
        return jnp.concatenate([jnp.where(first, v, 0.0), jnp.where(first, 0.0, v)], axis=0).astype(BF16)

    def per_head(v, f):
        return jnp.concatenate([f(v[:, :src]), f(v[:, src:])], axis=1)

    def dot_t(m, n):
        return lax.dot_general(m, n, (((1,), (1,)), ((), ())), preferred_element_type=F32)

    def t_dot(m, n):
        return lax.dot_general(m, n, (((0,), (0,)), ((), ())), preferred_element_type=F32)

    def attend(c):
        lanes = pl.ds(pl.multiple_of(c * 128, 128), 128)

        def one(b, carry):
            at_rows = sequence(b)
            kv_b = own_part[c, at_rows, :]
            rs_arrived(c, b)
            for j in range(3):
                kv_b = kv_b + rs_recv[c, j, at_rows, :].astype(F32)
            keys = two_heads(kv_b[:, :128].astype(BF16).astype(F32))
            values = two_heads(kv_b[:, 128:].astype(BF16).astype(F32))
            query, cotan = q_ref[b, :, lanes], og_ref[b, :, lanes]
            expo = jnp.where(place < len_ref[b], jnp.exp(dot_t(query, keys) * SCALE), 0.0)
            probs = per_head(expo, lambda e: e / jnp.sum(e, axis=-1, keepdims=True))
            probs_b = probs.astype(BF16)
            att_ref[b, :, lanes] = jnp.dot(probs_b, values, preferred_element_type=F32).astype(BF16)
            dprob = dot_t(cotan, values)
            delta = per_head(
                probs * dprob, lambda e: jnp.broadcast_to(jnp.sum(e, axis=-1, keepdims=True), e.shape)
            )
            dscore = (probs * (dprob - delta) * SCALE).astype(BF16)
            gq_ref[b, :, lanes] = jnp.dot(dscore, keys, preferred_element_type=F32).astype(BF16)
            dkey, dvalue = t_dot(dscore, query), t_dot(probs_b, cotan)
            dkv = jnp.concatenate(
                [jnp.where(first, dkey[:src], dkey[src:]), jnp.where(first, dvalue[:src], dvalue[src:])], axis=1
            ).astype(BF16)
            ag[c, x, at_rows, :] = dkv
            for j in (1, 0, 2):
                ag_copy(c, j, b).start()
            product = dkv.astype(F32) * kv_b
            racc[at_rows, :] = racc[at_rows, :] + (product[:, :128] + product[:, 128:])
            return carry

        lax.fori_loop(0, batches, one, 0)

    def back(chunks):
        for c in chunks:
            for b in range(batches):
                ag_arrived(c, b)

        def one(r, carry):
            term = dot_t(ag[chunks[0]].reshape(4 * rows, cols), wg[r, chunks[0]])
            for c in chunks[1:]:
                term = term + dot_t(ag[c].reshape(4 * rows, cols), wg[r, c])
            for xs in range(4):
                mine = term[xs * rows : (xs + 1) * rows]
                dn[xs, r] = mine if chunks[0] == 0 else dn[xs, r] + mine
            return carry

        lax.fori_loop(0, 4, one, 0)

    project(0)
    hop(1, 2)
    w_send(3)
    project(1)
    attend(0)
    hop(2, 2)
    attend(1)
    hop(0, 3)
    back((0,))
    project(2)
    hop(1, 3)
    back((1,))
    hop(2, 3)
    attend(2)
    project(3)
    attend(3)
    reduce_start(8, total_lanes(racc[...]))
    last = CHUNKS - 1
    for r in range(4):
        turned[r] = wg[r, last].T
    back((2,))

    SHARES = ((0, src), (src, src // 2), (src + src // 2, src - src // 2))

    def share(b):
        return pl.ds(*SHARES[b])

    def d1_copy(b, k):
        part = share(b)
        return copy(
            core_send.at[k, :, part], core_recv.at[k, :, part], d1_s.at[0], d1_r.at[b, k], at(core_=other)
        )

    SLOT = {1: 0, 3: 1, 2: 2}

    def d2_copy(b, k):
        halves = 0 if k == 2 else slice(None)
        part, slot, two = share(b), SLOT[k], int(k == 2)
        return copy(
            y_send.at[halves, slot, part], y_recv.at[halves, slot, part], d2_s.at[two], d2_r.at[two, b],
            at(y_=rotate(y, k, NY)),
        )

    def d2_arrived(b):
        pieces = y_recv.at[:, pl.ds(0, 2), share(b)]
        copy(pieces, pieces, d2_s.at[0], d2_r.at[0, b], at(core_=other)).wait_recv()
        d2_copy(b, 2).wait_recv()

    def whole(b, xs, k):
        part = share(b)
        r = lax.rem(y + k + NZ - zh, NZ)
        return dn[xs, r, part, :] + jnp.dot(ag[last, xs, part, :], turned[r], preferred_element_type=F32)

    def dz_copy(b):
        part = share(b)
        return copy(z_send.at[part], z_recv.at[part], dz_s.at[b], dz_r.at[b], at(zl_=1 - zl))

    def chip_sum(b, half, k):
        return whole(b, core + 2 * half, k) + core_recv[k, half, share(b), :].astype(F32)

    def cores(b):
        if b < batches:
            ag_arrived(last, b)
        part = share(b)
        for k in (2, 1, 3, 0):
            for half in (0, 1):
                core_send[k, half, part, :] = whole(b, other + 2 * half, k).astype(BF16)
            d1_copy(b, k).start()
        d1_copy(b, 2).wait_recv()
        z_send[part, :] = chip_sum(b, 1 - zl, 2).astype(BF16)
        dz_copy(b).start()

    def one_step(b):
        for k in (1, 3):
            d1_copy(b, k).wait_recv()
            for half in (0, 1):
                y_send[half, SLOT[k], share(b), :] = chip_sum(b, half, k).astype(BF16)
            d2_copy(b, k).start()

    def two_steps(b):
        part = share(b)
        v = chip_sum(b, zl, 2)
        dz_copy(b).wait_recv()
        y_send[0, 2, part, :] = (v + z_recv[part, :].astype(F32)).astype(BF16)
        d2_copy(b, 2).start()

    cores(0)
    one_step(0)
    reduce_zl(8)
    cores(1)
    two_steps(0)
    reduce_y(8)
    one_step(1)
    cores(2)
    two_steps(1)
    one_step(2)
    two_steps(2)
    for b in range(3):
        d1_copy(b, 0).wait_recv()
        for half in (0, 1):
            y_own[half, share(b), :] = chip_sum(b, half, 0)

    def d3_copy(b, half):
        part = share(b)
        to = (y, zh * 4 + core + 2 * half, x)
        return copy(fin_send.at[half, part], fin.at[zl, part], d3_s.at[b, half], d3_r.at[b, zl], to)

    def stays(half):
        return jnp.logical_and(home, x // 2 == half)

    def deliver(b):
        part = share(b)
        d2_arrived(b)
        for half in (0, 1):
            v = y_own[half, part, :]
            for k in (1, 3):
                v = v + y_recv[half, SLOT[k], part, :].astype(F32)
            v = v + jnp.where(zl == half, y_recv[0, 2, part, :].astype(F32), 0.0)
            fin_send[half, part, :] = v.astype(BF16)

            @pl.when(stays(half))
            def _():
                pltpu.make_async_copy(fin_send.at[half, part], fin.at[zl, part], d3_r.at[b, zl]).start()

            @pl.when(jnp.logical_not(stays(half)))
            def _():
                d3_copy(b, half).start()

    def weighed(v, half, k):
        hidden = raw[half, rotate(y, k, NY), :rows, :].astype(F32) * wide(piece_inv[half])
        return jnp.sum(v.astype(F32) * hidden, axis=0, keepdims=True)

    def folded(v):
        lanes = [v[:, i : i + 128] for i in range(0, feats, 128)]
        return jnp.concatenate(lanes + lanes, axis=0)

    def gz_copy(k):
        return copy(gz.at[zh], gz.at[zh], gz_s.at[k - 1], gz_r.at[k - 1], at(zh_=rotate(zh, k, NZ)))

    def gz_arrival(k):
        piece = gz.at[rotate(zh, 4 - k, NZ)]
        return copy(piece, piece, gz_s.at[k - 1], gz_r.at[k - 1], at(zh_=rotate(zh, k, NZ)))

    def gy_copy(k):
        return copy(gz.at[4, k], gy.at[y], gy_s.at[k - 1], gy_r.at[k - 1], at(y_=rotate(y, k, NY)))

    def gy_arrival(k):
        piece = gy.at[rotate(y, 4 - k, NY)]
        return copy(piece, piece, gy_s.at[k - 1], gy_r.at[k - 1], at(y_=rotate(y, k, NY)))

    def gx_copy(x_):
        place = 2 * zl + core
        return copy(gy.at[4], gx.at[place], gx_s.at[x_], gx_r.at[place], (y, zh * 4 + x_, x))

    gz[zh, 0] = folded(weighed(y_own[0], 0, 0) + weighed(y_own[1], 1, 0))
    for k in (1, 3):
        gz[zh, k] = folded(weighed(y_send[0, SLOT[k]], 0, k) + weighed(y_send[1, SLOT[k]], 1, k))
    gz[zh, 2] = folded(weighed(y_send[0, 2], zl, 2))
    for k in (1, 2, 3):
        gz_copy(k).start()
    deliver(0)
    inv = inv_ref[...]
    rsum_ref[...] = spread(reduce_end(8)[:1]) * inv * inv / width
    for k in (1, 2, 3):
        gz_arrival(k).wait_recv()
    gz[4] = (gz[0] + gz[1]) + (gz[2] + gz[3])
    gy[y] = gz[4, 0]
    for k in (1, 2, 3):
        gy_copy(k).start()

    def all_sent(pieces, sem, arrived):
        copy(pieces, pieces, sem, arrived, at(core_=other)).wait_send()

    all_sent(through, w_s.at[0], w_r.at[0, 0, 0])
    for stage in range(1, 5):
        all_sent(through_half, w_s.at[stage], w_r.at[stage, 0, 0])
    all_sent(part_send, rs_s.at[0], rs_r.at[0, 0])
    all_sent(ag.at[:, pl.ds(0, 3)], ag_s.at[0], ag_r.at[0, 0])
    all_sent(raw.at[0], s2_s.at[0], s2_r.at[0, 0])
    all_sent(raw.at[0, pl.ds(0, 2)], s2f_s.at[0], s2f_r.at[0, 0])
    s3_all().wait_send()
    all_sent(core_send, d1_s.at[0], d1_r.at[0, 0])

    @pl.when(jnp.logical_not(home))
    def _():
        s1_near.wait_send()

    for k in (1, 2, 3):
        xt_copy(k).wait_send()
    deliver(1)
    deliver(2)

    def owned(b):
        part = share(b)
        for k in (0, 1):
            copy(fin_send.at[0, part], fin.at[k, part], d3_s.at[b, 0], d3_r.at[b, k], at(core_=other)).wait_recv()
        dnormed = fin[0, part, :].astype(F32) + fin[1, part, :].astype(F32)
        own_gain = ext[rows : rows + 16, :].astype(F32)[:1]
        gs_ref[part, :] = own_gain * (wide(inv_ref[part, :]) * dnormed) - ext[part, :].astype(F32) * wide(
            rsum_ref[part, :]
        )

    for k in (1, 2, 3):
        gy_arrival(k).wait_recv()
    gy[4] = (gy[0] + gy[1]) + (gy[2] + gy[3])
    for x_ in range(NX):
        itself = jnp.logical_and(home, x == x_)

        @pl.when(itself)
        def _():
            place = 2 * zl + core
            pltpu.make_async_copy(gy.at[4], gx.at[place], gx_r.at[place]).start()

        @pl.when(jnp.logical_not(itself))
        def _():
            gx_copy(x_).start()

    owned(0)
    owned(1)
    owned(2)

    all_sent(y_send.at[:, pl.ds(0, 2)], d2_s.at[0], d2_r.at[0, 0])
    all_sent(y_send.at[0, 2], d2_s.at[1], d2_r.at[1, 0])
    for b in range(3):
        dz_copy(b).wait_send()
        for half in (0, 1):

            @pl.when(jnp.logical_not(stays(half)))
            def _():
                d3_copy(b, half).wait_send()

    for k in (1, 2, 3):
        gz_copy(k).wait_send()
        gy_copy(k).wait_send()
    for x_ in range(NX):

        @pl.when(jnp.logical_not(jnp.logical_and(home, x == x_)))
        def _():
            gx_copy(x_).wait_send()

    for k in range(4):
        copy(gy.at[4], gx.at[k], gx_s.at[0], gx_r.at[k], at(core_=other)).wait_recv()
    total = (gx[0] + gx[1]) + (gx[2] + gx[3])
    gg_ref[...] = jnp.concatenate([total[i : i + 1] for i in range(feats // 128)], axis=1)


def per_device(states, gain, kv_weight, queries, out_grad, src_len):
    batches, src, feats = states.shape
    tgt, heads_cols = queries.shape[2:]
    rows = batches * src
    cols = 2 * heads_cols // CHUNKS
    w = kv_weight.reshape(feats, 2 * heads_cols)
    gains = jnp.broadcast_to(gain[None, :], (16, feats))
    vmem = pl.BlockSpec(memory_space=pltpu.VMEM)
    dma = pltpu.SemaphoreType.DMA
    out = pl.pallas_call(
        kernel,
        out_shape=(
            jax.ShapeDtypeStruct((batches, tgt, heads_cols), BF16),
            jax.ShapeDtypeStruct((batches, tgt, heads_cols), BF16),
            jax.ShapeDtypeStruct((rows, feats), F32),
            jax.ShapeDtypeStruct((1, feats), F32),
        ),
        in_specs=[pl.BlockSpec(memory_space=pl.ANY)] * 6,
        out_specs=[vmem] * 4,
        scratch_shapes=[
            pltpu.SMEM((batches,), jnp.int32),
            pltpu.VMEM((rows + 16, feats), BF16),
            pltpu.VMEM((batches, tgt, heads_cols), BF16),
            pltpu.VMEM((batches, tgt, heads_cols), BF16),
            pltpu.VMEM((4, CHUNKS, feats, cols), BF16),
            pltpu.VMEM((2, CHUNKS, feats, cols), BF16),
            pltpu.VMEM((2, CHUNKS, feats // 2, cols), BF16),
            pltpu.VMEM((4, cols, feats), BF16),
            pltpu.VMEM((2, 4, rows + 16, feats), BF16),
            pltpu.VMEM((4, 4, rows, feats), BF16),
            pltpu.VMEM((CHUNKS, rows, cols), F32),
            pltpu.VMEM((CHUNKS, 3, rows, cols), BF16),
            pltpu.VMEM((CHUNKS, 3, rows, cols), BF16),
            pltpu.VMEM((CHUNKS, 4, rows, cols), BF16),
            pltpu.VMEM((4, 4, rows, feats), F32),
            pltpu.VMEM((4, 2, rows, feats), BF16),
            pltpu.VMEM((4, 2, rows, feats), BF16),
            pltpu.VMEM((rows, feats), BF16),
            pltpu.VMEM((rows, feats), BF16),
            pltpu.VMEM((2, 3, rows, feats), BF16),
            pltpu.VMEM((2, 3, rows, feats), BF16),
            pltpu.VMEM((2, rows, feats), F32),
            pltpu.VMEM((2, rows, feats), BF16),
            pltpu.VMEM((2, rows, feats), BF16),
            pltpu.VMEM((rows, 128), F32),
            pltpu.VMEM((16, 8, rows), F32),
            pltpu.VMEM((4, 8, rows), F32),
            pltpu.VMEM((5, 4, 8, 128), F32),
            pltpu.VMEM((5, 8, 128), F32),
            pltpu.VMEM((4, 8, 128), F32),
            pltpu.VMEM((rows, 128), F32),
            pltpu.VMEM((2, rows, 128), F32),
            pltpu.VMEM((rows, 128), F32),
            dma((6,)),
            dma((5,)), dma((5, 2, CHUNKS)),
            dma((2,)), dma((2,)),
            dma((1,)), dma((2, 2)), dma((1,)), dma((2, 2)),
            dma((1,)), dma((1,)),
            dma((1,)), dma((CHUNKS, 2)),
            dma((1,)), dma((CHUNKS, 2)),
            dma((1,)), dma((3, 4)),
            dma((3,)), dma((3,)),
            dma((2,)), dma((2, 3)),
            dma((3, 2)), dma((3, 2)),
            dma((16,)), dma((16,)),
            dma((3,)), dma((3,)),
            dma((3,)), dma((3,)),
            dma((3,)), dma((3,)),
            dma((4,)), dma((4,)),
        ],
        compiler_params=pltpu.CompilerParams(
            collective_id=1, has_side_effects=True, vmem_limit_bytes=52 * 2**20
        ),
        name="cross_attention",
    )(
        w, states.reshape(rows, feats), gains, queries[0], out_grad[0], src_len
    )
    attended, grad_q, grad_states, grad_gain = out
    return attended[None], grad_q[None], grad_states.reshape(batches, src, feats), grad_gain[0]


def solution(mesh):
    return jax.shard_map(
        per_device,
        mesh=mesh,
        in_specs=(
            P("dp", None, ("section", "tensor")),
            P(("section", "tensor")),
            P("section", "dp", None, "tensor"),
            P("section", "dp", None, "tensor"),
            P("section", "dp", None, "tensor"),
            P("dp"),
        ),
        out_specs=(
            P("section", "dp", None, "tensor"),
            P("section", "dp", None, "tensor"),
            P("dp", None, ("section", "tensor")),
            P(("section", "tensor")),
        ),
        check_vma=False,
    )
```
